32 devices in a mesh: dp: 4 (over y, core), seq: 4 (over z), mp: 2 (over x).
Axes of the slice: x: 2, y: 2, z: 4, core: 2. Of those that a mesh axis runs over, the one named last changes fastest.
Arguments:
- tokens: bfloat16 [8192, 2048], P(('dp', 'seq')), may hold values from -6 to 6
- doc_lengths: int32 [4, 4], P('dp'), may hold values from 1 to 2048, as said below
- norm_gain: float32 [2048], replicated, may hold values from 0.1 to 1.9
- w_y: bfloat16 [2048, 2560], P(('dp', 'seq'), 'mp'), may hold values from -0.125 to 0.125
- w_x: bfloat16 [2048, 2560], P(('dp', 'seq'), 'mp'), may hold values from -0.125 to 0.125
- gate_a: bfloat16 [10, 256, 256], P('mp'), may hold values from -0.375 to 0.375
- gate_i: bfloat16 [10, 256, 256], P('mp'), may hold values from -0.375 to 0.375
- bias_a: float32 [2560], P('mp'), may hold values from -4 to 4
- bias_i: float32 [2560], P('mp'), may hold values from -4 to 4
- conv_w: float32 [4, 2560], P(None, 'mp'), may hold values from -3 to 3
- conv_b: float32 [2560], P('mp'), may hold values from -3 to 3
- decay_param: float32 [2560], P('mp'), may hold values from 3 to 13
- w_out: bfloat16 [2048, 2560], P(('dp', 'seq'), 'mp'), may hold values from -0.25 to 0.25
- mlp_gain: float32 [2048], replicated, may hold values from 0.1 to 1.9
- w_gate: bfloat16 [2048, 6144], P(('dp', 'seq'), 'mp'), may hold values from -0.125 to 0.125
- w_up: bfloat16 [2048, 6144], P(('dp', 'seq'), 'mp'), may hold values from -0.125 to 0.125
- w_down: bfloat16 [2048, 6144], P(('dp', 'seq'), 'mp'), may hold values from -0.15625 to 0.15625
- cotangent: bfloat16 [8192, 2048], P(('dp', 'seq')), may hold values from -6 to 6
Outputs:
- output: bfloat16 [8192, 2048], P(('dp', 'seq'))
- input_grad: float32 [8192, 2048], P(('dp', 'seq'))
- grad_norm_gain: float32 [2048], replicated
- grad_w_y: float32 [2048, 2560], P(('dp', 'seq'), 'mp')
- grad_w_x: float32 [2048, 2560], P(('dp', 'seq'), 'mp')
- grad_gate_a: float32 [10, 256, 256], P('mp')
- grad_gate_i: float32 [10, 256, 256], P('mp')
- grad_bias_a: float32 [2560], P('mp')
- grad_bias_i: float32 [2560], P('mp')
- grad_conv_w: float32 [4, 2560], P(None, 'mp')
- grad_conv_b: float32 [2560], P('mp')
- grad_decay_param: float32 [2560], P('mp')
- grad_w_out: float32 [2048, 2560], P(('dp', 'seq'), 'mp')
- grad_mlp_gain: float32 [2048], replicated
- grad_w_gate: float32 [2048, 6144], P(('dp', 'seq'), 'mp')
- grad_w_up: float32 [2048, 6144], P(('dp', 'seq'), 'mp')
- grad_w_down: float32 [2048, 6144], P(('dp', 'seq'), 'mp')
The draws below stay inside these ranges and needn't reach their ends.
Inputs may be any that keep to these rules, and one draw needn't show every extreme that they name: `doc_lengths`: each row gives, in order, the lengths of the 4 documents packed into one sequence, and sums to 2048.
All inputs are finite; a program needn't handle non-finite values.
Results may differ from the reference program's by a relative error of at most 0.0088.
Values may be sent and summed in bfloat16 or wider, within the bound.
A program may use at most 384 MiB of HBM per device.

```python
import jax
import jax.numpy as jnp
from jax import lax

D = 2048
WIDTH = 2560
HEADS = 10
FF = 6144
CONV = 4
BLOCK = 256
TOK_DEV = 512
DOCS = 4
LENGTH = 2048
SEQS = 4
TOKENS = 8192


def draw_doc_lengths(key, part):
    key = jax.random.fold_in(key, 11)
    key_len, key_pick = jax.random.split(key)
    short = jax.random.randint(key_len, (SEQS, DOCS), 1, TOK_DEV // DOCS + 1)
    pick = jax.random.randint(key_pick, (SEQS, 1), 0, DOCS)
    is_long = jnp.arange(DOCS, dtype=jnp.int32)[None, :] == pick
    others = jnp.sum(jnp.where(is_long, 0, short), axis=1, keepdims=True)
    return jnp.where(is_long, LENGTH - others, short).astype(jnp.int32)


def draw_decay_param(key, part):
    key = jax.random.fold_in(key, 23)
    key_pick, key_rate = jax.random.split(key)
    slow_tenths = 5
    slow = jax.random.randint(key_pick, (WIDTH,), 0, 10) < slow_tenths
    spread = jax.random.uniform(key_rate, (WIDTH,), jnp.float32)
    slow_rate = 0.05 / LENGTH * 10.0 ** spread
    fast_rate = 0.5 / LENGTH * (0.06 * LENGTH) ** spread
    rate = jnp.where(slow, slow_rate, fast_rate)
    return (-jnp.log(jnp.expm1(rate))).astype(jnp.float32)


def spiked(entries, key, source, target, parts, factor):
    owner, partner = [(jnp.arange(entries.shape[dim]) // (entries.shape[dim] // parts)).reshape([-1 if axis == dim else 1 for axis in range(entries.ndim)]) for dim in (source, target)]
    chosen = jax.random.permutation(key, parts)[partner]
    strong = (owner == chosen) | (owner == (partner + parts // 2) % parts)
    return jnp.where(strong, factor * entries, entries)


def level_of(stream_key, dims, cuts, low, high):
    level = 1.0
    for dim, blocks in cuts:
        draws = jax.random.uniform(jax.random.fold_in(jax.random.fold_in(stream_key, 6), dim), (blocks,), jnp.float32, low / len(cuts), high / len(cuts))
        level = level * jnp.repeat(jnp.exp(draws), dims[dim] // blocks).reshape((-1,) + (1,) * (len(dims) - 1 - dim))
    return level


def centred(rng, shape, scale, reach, pieces=(), kind=jnp.bfloat16):
    entries = jax.random.normal(rng, shape, jnp.float32) * scale
    if len(pieces) > 0:
        entries = level_of(rng, shape, pieces, -0.22, 0.18) * entries
    return jnp.clip(entries, min=-reach, max=reach).astype(kind)


def gaussian_with(key, dims, width, most, cuts, heavy, kind=jnp.bfloat16):
    entries = width * jax.random.normal(key, dims, jnp.float32)
    if cuts:
        entries = entries * level_of(key, dims, cuts, -0.22, 0.18)
    return jnp.clip(spiked(entries, jax.random.fold_in(key, 3), *heavy), -most, most).astype(kind)


def setup_inputs(seed: int = 0) -> dict:
    key_of = jax.random.split(jax.random.key(seed), 19)
    tokens = centred(key_of[0], (TOKENS, D), 1.0, 6.0, ((0, 16),))
    doc_lengths = draw_doc_lengths(jax.random.fold_in(key_of[18], 71), 0)
    norm_gain = jnp.clip(1.0 + 0.18 * jax.random.normal(key_of[2], (D,), jnp.float32), 0.1, 1.9)
    w_y = centred(key_of[3], (D, WIDTH), D ** -0.5, 0.125, ((0, 16), (1, 2)))
    w_x = centred(key_of[4], (D, WIDTH), D ** -0.5, 0.125, ((0, 16), (1, 2)))
    gate_a = centred(key_of[5], (HEADS, BLOCK, BLOCK), BLOCK ** -0.5, 0.375, ((0, 2),))
    gate_i = centred(key_of[6], (HEADS, BLOCK, BLOCK), BLOCK ** -0.5, 0.375, ((0, 2),))
    bias_a = centred(key_of[7], (WIDTH,), 1.0, 4.0, ((0, 2),), jnp.float32)
    bias_i = centred(key_of[8], (WIDTH,), 1.0, 4.0, ((0, 2),), jnp.float32)
    conv_w = centred(key_of[9], (CONV, WIDTH), 0.5, 3.0, ((1, 2),), jnp.float32)
    conv_b = centred(key_of[10], (WIDTH,), 0.5, 3.0, ((0, 2),), jnp.float32)
    decay_param = draw_decay_param(jax.random.fold_in(key_of[18], 71), 0)
    w_out = centred(key_of[12], (D, WIDTH), (WIDTH // 4) ** -0.5, 0.25, ((0, 16), (1, 2)))
    mlp_gain = jnp.clip(1.0 + 0.18 * jax.random.normal(key_of[13], (D,), jnp.float32), 0.1, 1.9)
    w_gate = centred(key_of[14], (D, FF), D ** -0.5, 0.125, ((0, 16), (1, 2)))
    w_up = centred(key_of[15], (D, FF), D ** -0.5, 0.125, ((0, 16), (1, 2)))
    w_down = centred(key_of[16], (D, FF), (FF // 4) ** -0.5, 0.15625, ((0, 16), (1, 2)))
    cotangent = gaussian_with(key_of[17], (TOKENS, D), 1.0, 6.0, ((0, 16),), (0, 1, 16, 2.0))
    return dict(tokens=tokens, doc_lengths=doc_lengths, norm_gain=norm_gain, w_y=w_y, w_x=w_x, gate_a=gate_a, gate_i=gate_i, bias_a=bias_a, bias_i=bias_i, conv_w=conv_w, conv_b=conv_b, decay_param=decay_param, w_out=w_out, mlp_gain=mlp_gain, w_gate=w_gate, w_up=w_up, w_down=w_down, cotangent=cotangent)


epsilon = 1e-06
decay_scale = 8.0
highest = lax.Precision.HIGHEST

@jax.custom_vjp
def low(v):
    return lax.optimization_barrier(v.astype(jnp.bfloat16)).astype(jnp.float32)

@jax.custom_vjp
def low_back(v):
    return v

def low_keep(v):
    return (low(v), None)

def low_pass(kept, grad):
    return (grad,)

def back_keep(v):
    return (v, None)

def back_low(kept, grad):
    return (low(grad),)
low.defvjp(low_keep, low_pass)
low_back.defvjp(back_keep, back_low)

def product(left, right):
    return jnp.dot(left, right, precision=highest, preferred_element_type=jnp.float32)

def normalize(values, gain):
    return values * lax.rsqrt(lax.optimization_barrier(jnp.mean(values * values, axis=-1, keepdims=True)) + epsilon) * gain

def compose(first_part, second_part):
    return (first_part[0] * second_part[0], second_part[0] * first_part[1] + second_part[1])

def gate_decay(gate_r, gate_x, conv_out, decay_param, bias_a, bias_i, keep_state):
    rate = jax.nn.sigmoid(gate_r + bias_a)
    input_gate = jax.nn.sigmoid(gate_x + bias_i)
    log_decay = -decay_scale * rate * jax.nn.softplus(-decay_param)
    decays = jnp.exp(log_decay) * keep_state
    drives = conv_out * input_gate * jnp.sqrt(-jnp.expm1(2.0 * log_decay))
    return (decays, drives)

def document_marks(lengths_row):
    position = jnp.arange(LENGTH, dtype=jnp.int32)
    starts = (jnp.cumsum(lengths_row) - lengths_row).astype(jnp.int32)
    resets = jnp.any(position[:, None] == starts[None, :], axis=1)
    doc_start = lax.optimization_barrier(jnp.max(jnp.where(starts[None, :] <= position[:, None], starts[None, :], 0), axis=1))
    keep_state = 1.0 - resets.astype(jnp.float32)[:, None]
    same_doc = jnp.stack([(position - offset >= doc_start).astype(jnp.float32) for offset in range(CONV)])[:, :, None]
    return (keep_state, same_doc)

def layer(tokens, keep_state, same_doc, norm_gain, w_y, w_x, gate_a, gate_i, bias_a, bias_i, conv_w, conv_b, decay_param, w_out, mlp_gain, w_gate, w_up, w_down):
    activations = low(normalize(tokens, norm_gain))
    pre_y = low_back(product(activations, w_y))
    conv_in = low(low_back(product(activations, w_x)))
    conv_out = conv_b
    for offset in range(CONV):
        shifted = jnp.pad(conv_in, ((offset, 0), (0, 0)))[:LENGTH]
        conv_out = conv_out + conv_w[offset] * shifted * same_doc[offset]
    conv_low = low(conv_out).reshape(LENGTH, HEADS, BLOCK)
    gate_r = low_back(jnp.einsum('thi,hij->thj', conv_low, gate_a, precision=highest).reshape(LENGTH, WIDTH))
    gate_x = low_back(jnp.einsum('thi,hij->thj', conv_low, gate_i, precision=highest).reshape(LENGTH, WIDTH))
    decays, drives = gate_decay(gate_r, gate_x, conv_out, decay_param, bias_a, bias_i, keep_state)
    states = lax.associative_scan(compose, (decays, drives))[1]
    mixed_rec = low(states * jax.nn.gelu(pre_y))
    middle = tokens + low_back(product(mixed_rec, w_out.T))
    activations_two = low(normalize(middle, mlp_gain))
    pre_gate = low_back(product(activations_two, w_gate))
    pre_up = low_back(product(activations_two, w_up))
    mixed_mlp = low(jax.nn.gelu(pre_gate) * pre_up)
    return middle + low_back(product(mixed_mlp, w_down.T))

def reference(tokens, doc_lengths, norm_gain, w_y, w_x, gate_a, gate_i, bias_a, bias_i, conv_w, conv_b, decay_param, w_out, mlp_gain, w_gate, w_up, w_down, cotangent):
    weights = tuple((item.astype(jnp.float32) for item in (norm_gain, w_y, w_x, gate_a, gate_i, bias_a, bias_i, conv_w, conv_b, decay_param, w_out, mlp_gain, w_gate, w_up, w_down)))

    def one_sequence(totals, inputs):
        seq_tokens, lengths_row, seq_cotangent = inputs
        keep_state, same_doc = document_marks(lengths_row)

        def forward(seq_in, *params):
            return layer(seq_in, keep_state, same_doc, *params)
        final, pull = jax.vjp(forward, seq_tokens.astype(jnp.float32), *weights)
        grads = pull(seq_cotangent.astype(jnp.float32))
        totals = tuple((total + grad for total, grad in zip(totals, grads[1:])))
        return (totals, (final.astype(jnp.bfloat16), grads[0]))
    start_totals = tuple((jnp.zeros_like(weight) for weight in weights))
    totals, (outputs, input_grads) = lax.scan(one_sequence, start_totals, (tokens.reshape(SEQS, LENGTH, D), doc_lengths, cotangent.reshape(SEQS, LENGTH, D)))
    return (outputs.reshape(TOKENS, D), input_grads.reshape(TOKENS, D), totals[0], totals[1], totals[2], totals[3], totals[4], totals[5], totals[6], totals[7], totals[8], totals[9], totals[10], totals[11], totals[12], totals[13], totals[14])
```

```python
import functools

import jax
import jax.numpy as jnp
from jax import lax
from jax.experimental import pallas as pl
from jax.experimental.pallas import tpu as pltpu
from jax.sharding import PartitionSpec as P

epsilon = 1e-06
decay_scale = 8.0
MESH = pl.DeviceIdType.MESH
VMEM_LIMIT = 60 * 2**20
SEGMENTS = 8
PAD = 8
CHUNKS = 4
bf16 = jnp.bfloat16
f32 = jnp.float32


def xor_permute(value, axis, bit):
    count = lax.axis_size(axis)
    return lax.ppermute(value, axis, [(source, source ^ bit) for source in range(count)])


def matmul(left, right):
    return jnp.dot(left, right, preferred_element_type=f32)


def contract(left, right):
    return lax.dot_general(left, right, (((1,), (1,)), ((), ())), preferred_element_type=f32)


def contract_rows(left, right):
    return lax.dot_general(left, right, (((0,), (0,)), ((), ())), preferred_element_type=f32)


def norm_scale(values):
    return lax.rsqrt(jnp.mean(values * values, axis=-1, keepdims=True) + epsilon)


def gelu_parts(y):
    c = 0.7978845608028654
    u = c * (y + 0.044715 * y * y * y)
    t = jnp.tanh(u)
    half = 0.5 * (1.0 + t)
    slope = half + 0.5 * y * (1.0 - t * t) * (c * (1.0 + 3.0 * 0.044715 * y * y))
    return y * half, slope


def one_minus_square(log_decay, decay):
    y = -2.0 * log_decay
    series = 1.0 - y * (1.0 / 8.0)
    for k in (7, 6, 5, 4, 3, 2):
        series = 1.0 - y * (1.0 / k) * series
    return jnp.where(y < 0.5, y * series, 1.0 - decay * decay)


def seq_barrier(nseq):
    dp, z, mp = (lax.axis_index(a) for a in ("dp", "seq", "mp"))
    barrier = pltpu.get_barrier_semaphore()
    for step in range(1, nseq):
        pl.semaphore_signal(
            barrier, inc=1, device_id=(dp, lax.rem(z + step, nseq), mp), device_id_type=MESH
        )
    pl.semaphore_wait(barrier, nseq - 1)


def to_seq(src, dst, send_sem, recv_sem, target):
    dp, mp = (lax.axis_index(a) for a in ("dp", "mp"))
    return pltpu.make_async_remote_copy(
        src_ref=src,
        dst_ref=dst,
        send_sem=send_sem,
        recv_sem=recv_sem,
        device_id=(dp, target, mp),
        device_id_type=MESH,
    )


LANES = 128


def put(ref, at, h, value):
    count = value.shape[1] // LANES
    for k in range(count):
        ref[h * count + k, at, :] = value[:, k * LANES : (k + 1) * LANES]


def take(ref, at, h, block):
    count = block // LANES
    return jnp.concatenate([ref[h * count + k, at, :] for k in range(count)], axis=1)


def side_by_side(parts):
    return jnp.concatenate(parts, axis=1)


def rec_forward_kernel(
    nseq, heads, block,
    px_ref, py_ref, marks_ref, ga_ref, gi_ref, vec_ref,
    mixed_ref, states_ref, pxe_ref, rate_ref, ig_ref, co_ref,
    a_s, b_s, msg, got, state_in, halo, halo_send, halo_recv, end_send, end_recv,
):
    rows, width = px_ref.shape
    seg = rows // SEGMENTS
    z = lax.axis_index("seq")
    seq_barrier(nseq)

    @pl.when(z < nseq - 1)
    def _():
        to_seq(px_ref.at[pl.ds(rows - PAD, PAD)], halo, halo_send, halo_recv, z + 1).start()

    def copy_rows(r, _):
        pxe_ref[pl.ds(PAD + r * seg, seg), :] = px_ref[pl.ds(r * seg, seg), :].astype(bf16).astype(f32)
        return 0

    lax.fori_loop(0, SEGMENTS, copy_rows, 0)

    @pl.when(z == 0)
    def _():
        halo[...] = jnp.zeros_like(halo)

    @pl.when(z > 0)
    def _():
        to_seq(px_ref.at[pl.ds(rows - PAD, PAD)], halo, halo_send, halo_recv, z).wait_recv()

    pxe_ref[pl.ds(0, PAD), :] = halo[...].astype(bf16).astype(f32)

    @pl.when(z < nseq - 1)
    def _():
        to_seq(px_ref.at[pl.ds(rows - PAD, PAD)], halo, halo_send, halo_recv, z).wait_send()

    def head(h, _):
        cols = pl.ds(pl.multiple_of(h * block, block), block)

        def part(r, _):
            at = pl.ds(pl.multiple_of(r * seg, seg), seg)
            window = pxe_ref[pl.ds(pl.multiple_of(r * seg, seg), seg + PAD), cols]
            conv_out = vec_ref[4:5, cols] + vec_ref[0:1, cols] * window[PAD:]
            for lag in (1, 2, 3):
                shifted = pltpu.roll(window, lag, 0)[PAD:]
                conv_out = conv_out + vec_ref[lag : lag + 1, cols] * shifted * marks_ref[lag, at, :]
            low = conv_out.astype(bf16)
            gate_r = matmul(low, ga_ref[h])
            gate_x = matmul(low, gi_ref[h])
            rate = jax.nn.sigmoid(gate_r + vec_ref[5:6, cols])
            ig = jax.nn.sigmoid(gate_x + vec_ref[6:7, cols])
            log_decay = -decay_scale * rate * vec_ref[7:8, cols]
            decay = jnp.exp(log_decay)
            mult = jnp.sqrt(one_minus_square(log_decay, decay))
            put(a_s, at, h, decay * marks_ref[0, at, :])
            put(b_s, at, h, conv_out * ig * mult)
            rate_ref[at, cols] = rate
            ig_ref[at, cols] = ig
            co_ref[at, cols] = conv_out
            return 0

        lax.fori_loop(0, SEGMENTS, part, 0)
        return 0

    lax.fori_loop(0, heads, head, 0)

    groups = width // LANES

    def turn(t, kept):
        at = pl.ds(t, SEGMENTS, stride=seg)
        result = []
        for g, (prefix, state) in enumerate(kept):
            decay = a_s[g, at, :]
            prefix = prefix * decay
            state = state * decay + b_s[g, at, :]
            a_s[g, at, :] = prefix
            b_s[g, at, :] = state
            result.append((prefix, state))
        return tuple(result)

    one, zero = jnp.ones((SEGMENTS, LANES), f32), jnp.zeros((SEGMENTS, LANES), f32)
    ends = lax.fori_loop(0, seg, turn, ((one, zero),) * groups)
    prefix, state = (side_by_side([end[k] for end in ends]) for k in (0, 1))
    total_a, total_b = prefix[0:1], state[0:1]
    for s in range(1, SEGMENTS):
        total_a, total_b = total_a * prefix[s : s + 1], total_b * prefix[s : s + 1] + state[s : s + 1]
    msg[0:1, :] = total_a
    msg[1:2, :] = total_b
    msg[2:PAD, :] = jnp.zeros((PAD - 2, width), f32)
    for step in range(1, nseq):

        @pl.when(z + step < nseq)
        def _():
            to_seq(msg, got.at[z], end_send.at[step - 1], end_recv.at[z], z + step).start()

    state_in[...] = jnp.zeros_like(state_in)
    for source in range(nseq - 1):

        @pl.when(source < z)
        def _():
            to_seq(msg, got.at[source], end_send.at[0], end_recv.at[source], z).wait_recv()
            state_in[...] = got[source, 0:1, :] * state_in[...] + got[source, 1:2, :]

    carry = state_in[...]
    states_ref[pl.ds(0, PAD), :] = jnp.broadcast_to(carry, (PAD, width))
    for s in range(SEGMENTS):
        halo[s : s + 1, :] = carry
        carry = prefix[s : s + 1] * carry + state[s : s + 1]

    def finish(i, _):
        s, h = i // heads, lax.rem(i, heads)
        cols = pl.ds(pl.multiple_of(h * block, block), block)
        at = pl.ds(pl.multiple_of(s * seg, seg), seg)
        states = take(b_s, at, h, block) + take(a_s, at, h, block) * halo[pl.ds(s, 1), cols]
        states_ref[pl.ds(pl.multiple_of(PAD + s * seg, PAD), seg), cols] = states
        mixed_ref[at, cols] = (states * gelu_parts(py_ref[at, cols])[0]).astype(bf16)
        return 0

    lax.fori_loop(0, SEGMENTS * heads, finish, 0)
    for step in range(1, nseq):

        @pl.when(z + step < nseq)
        def _():
            to_seq(msg, got.at[z], end_send.at[step - 1], end_recv.at[z], z).wait_send()


def rec_forward(nseq, px, py, marks, gate_a, gate_i, vectors):
    rows, width = px.shape
    heads, block = gate_a.shape[:2]
    vmem = pl.BlockSpec(memory_space=pltpu.VMEM)
    big = jax.ShapeDtypeStruct((rows, width), f32)
    ext = jax.ShapeDtypeStruct((rows + PAD, width), f32)
    small = pltpu.VMEM((PAD, width), f32)
    dma = pltpu.SemaphoreType.DMA
    return pl.pallas_call(
        functools.partial(rec_forward_kernel, nseq, heads, block),
        out_shape=(jax.ShapeDtypeStruct((rows, width), bf16), ext, ext, big, big, big),
        in_specs=[vmem] * 6,
        out_specs=[vmem] * 6,
        scratch_shapes=[
            pltpu.VMEM((width // LANES, rows, LANES), f32),
            pltpu.VMEM((width // LANES, rows, LANES), f32),
            small,
            pltpu.VMEM((nseq, PAD, width), f32),
            pltpu.VMEM((1, width), f32),
            small,
            dma, dma, dma((nseq - 1,)), dma((nseq,)),
        ],
        compiler_params=pltpu.CompilerParams(
            collective_id=1, has_side_effects=True, vmem_limit_bytes=VMEM_LIMIT
        ),
        name="rec_forward",
    )(px, py, marks, gate_a, gate_i, vectors)


def rec_backward_kernel(
    nseq, heads, block,
    gm_ref, py_ref, states_ref, pxe_ref, rate_ref, ig_ref, co_ref, marks_ref, ga_ref, gi_ref, vec_ref,
    gpy_ref, gpx_ref, gga_ref, ggi_ref, sums_ref,
    a_s, b_s, w_s, gc_s, gr_s, gx_s, msg, got, grad_in, carry_s, head_s, halo_send, halo_recv, end_send, end_recv,
):
    rows, width = gm_ref.shape
    seg = rows // SEGMENTS
    z = lax.axis_index("seq")
    seq_barrier(nseq)

    def first(i, _):
        s, h = i // heads, lax.rem(i, heads)
        cols = pl.ds(pl.multiple_of(h * block, block), block)
        at = pl.ds(pl.multiple_of(s * seg, seg), seg)
        gelu, slope = gelu_parts(py_ref[at, cols])
        gm = gm_ref[at, cols]
        states = states_ref[pl.ds(pl.multiple_of(PAD + s * seg, PAD), seg), cols]
        gpy_ref[at, cols] = (gm * states * slope).astype(bf16)
        put(b_s, at, h, gm * gelu)
        put(a_s, at, h, jnp.exp(-decay_scale * rate_ref[at, cols] * vec_ref[7:8, cols]) * marks_ref[0, at, :])
        return 0

    lax.fori_loop(0, SEGMENTS * heads, first, 0)

    groups = width // LANES

    def turn(i, kept):
        at = pl.ds(seg - 1 - i, SEGMENTS, stride=seg)
        result = []
        for g, (suffix, owed) in enumerate(kept):
            decay = a_s[g, at, :]
            carry = b_s[g, at, :] + owed
            b_s[g, at, :] = carry
            w_s[g, at, :] = suffix
            result.append((suffix * decay, carry * decay))
        return tuple(result)

    one, zero = jnp.ones((SEGMENTS, LANES), f32), jnp.zeros((SEGMENTS, LANES), f32)
    ends = lax.fori_loop(0, seg, turn, ((one, zero),) * groups)
    suffix, owed = (side_by_side([end[k] for end in ends]) for k in (0, 1))
    last = SEGMENTS - 1
    total_w, total_g = suffix[last:], owed[last:]
    for s in range(last - 1, -1, -1):
        total_w, total_g = total_w * suffix[s : s + 1], total_g * suffix[s : s + 1] + owed[s : s + 1]
    msg[0:1, :] = total_w
    msg[1:2, :] = total_g
    msg[2:PAD, :] = jnp.zeros((PAD - 2, width), f32)
    for step in range(1, nseq):

        @pl.when(z >= step)
        def _():
            to_seq(msg, got.at[z], end_send.at[step - 1], end_recv.at[z], z - step).start()

    grad_in[...] = jnp.zeros_like(grad_in)
    for source in range(nseq - 1, 0, -1):

        @pl.when(source > z)
        def _():
            to_seq(msg, got.at[source], end_send.at[0], end_recv.at[source], z).wait_recv()
            grad_in[...] = got[source, 0:1, :] * grad_in[...] + got[source, 1:2, :]

    carry = grad_in[...]
    for s in range(last, -1, -1):
        carry_s[s : s + 1, :] = carry
        carry = suffix[s : s + 1] * carry + owed[s : s + 1]

    def fold(value):
        return jnp.sum(value.reshape(seg // 8, 8, block), axis=0)

    def head(h, _):
        cols = pl.ds(pl.multiple_of(h * block, block), block)
        shrink = vec_ref[7:8, cols]

        def part(s, sums):
            at = pl.ds(pl.multiple_of(s * seg, seg), seg)
            ahead = pl.ds(pl.multiple_of(s * seg, seg), seg + PAD)
            carry = take(b_s, at, h, block) + take(w_s, at, h, block) * carry_s[pl.ds(s, 1), cols]
            before = pltpu.roll(states_ref[ahead, cols], 1, 0)[PAD:]
            rate, ig, conv_out = rate_ref[at, cols], ig_ref[at, cols], co_ref[at, cols]
            log_decay = -decay_scale * rate * shrink
            decay = jnp.exp(log_decay)
            mult = jnp.sqrt(one_minus_square(log_decay, decay))
            gated = carry * conv_out * ig
            grad_log = carry * before * decay * marks_ref[0, at, :] - gated * (decay * decay) / mult
            spread = grad_log * decay_scale * rate
            grad_r = -spread * shrink * (1.0 - rate)
            grad_x = gated * mult * (1.0 - ig)
            low_r, low_x = grad_r.astype(bf16), grad_x.astype(bf16)
            gr_s[at, :] = low_r
            gx_s[at, :] = low_x
            grad_conv = carry * ig * mult + contract(low_r, ga_ref[h]) + contract(low_x, gi_ref[h])
            gc_s[at, cols] = grad_conv
            window = pxe_ref[ahead, cols]
            terms = [grad_r, grad_x, spread, grad_conv, grad_conv * window[PAD:]]
            for lag in (1, 2, 3):
                terms.append(grad_conv * marks_ref[lag, at, :] * pltpu.roll(window, lag, 0)[PAD:])
            return tuple(total + fold(term) for total, term in zip(sums, terms))

        sums = lax.fori_loop(
            0, SEGMENTS, part, tuple(jnp.zeros((8, block), f32) for _ in range(8))
        )
        for k, total in enumerate(sums):
            sums_ref[k : k + 1, cols] = jnp.sum(total, axis=0, keepdims=True)
        low = co_ref[:, cols].astype(bf16)
        gga_ref[h] = contract_rows(low, gr_s[...])
        ggi_ref[h] = contract_rows(low, gx_s[...])
        return 0

    lax.fori_loop(0, heads, head, 0)
    head_s[...] = gc_s[pl.ds(0, PAD), :]

    @pl.when(z > 0)
    def _():
        to_seq(head_s, gc_s.at[pl.ds(rows, PAD)], halo_send, halo_recv, z - 1).start()

    @pl.when(z < nseq - 1)
    def _():
        to_seq(head_s, gc_s.at[pl.ds(rows, PAD)], halo_send, halo_recv, z).wait_recv()

    @pl.when(z == nseq - 1)
    def _():
        gc_s[pl.ds(rows, PAD), :] = jnp.zeros((PAD, width), f32)

    def final(i, _):
        s, h = i // heads, lax.rem(i, heads)
        cols = pl.ds(pl.multiple_of(h * block, block), block)
        at = pl.ds(pl.multiple_of(s * seg, seg), seg)
        ahead = pl.ds(pl.multiple_of(s * seg, seg), seg + PAD)
        owed = gc_s[ahead, cols]
        grad = vec_ref[0:1, cols] * owed[:seg]
        for lag in (1, 2, 3):
            shifted = pltpu.roll(owed * marks_ref[lag, ahead, :], seg + PAD - lag, 0)[:seg]
            grad = grad + vec_ref[lag : lag + 1, cols] * shifted
        gpx_ref[at, cols] = grad.astype(bf16)
        return 0

    lax.fori_loop(0, SEGMENTS * heads, final, 0)

    @pl.when(z > 0)
    def _():
        to_seq(head_s, gc_s.at[pl.ds(rows, PAD)], halo_send, halo_recv, z).wait_send()

    for step in range(1, nseq):

        @pl.when(z >= step)
        def _():
            to_seq(msg, got.at[z], end_send.at[step - 1], end_recv.at[z], z).wait_send()


def rec_backward(nseq, gm, py, states, pxe, rate, ig, co, marks, gate_a, gate_i, vectors):
    rows, width = gm.shape
    heads, block = gate_a.shape[:2]
    vmem = pl.BlockSpec(memory_space=pltpu.VMEM)
    low = jax.ShapeDtypeStruct((rows, width), bf16)
    gates = jax.ShapeDtypeStruct(gate_a.shape, f32)
    small = pltpu.VMEM((PAD, width), f32)
    dma = pltpu.SemaphoreType.DMA
    return pl.pallas_call(
        functools.partial(rec_backward_kernel, nseq, heads, block),
        out_shape=(low, low, gates, gates, jax.ShapeDtypeStruct((8, width), f32)),
        in_specs=[vmem] * 11,
        out_specs=[vmem] * 5,
        scratch_shapes=[
            pltpu.VMEM((width // LANES, rows, LANES), f32),
            pltpu.VMEM((width // LANES, rows, LANES), f32),
            pltpu.VMEM((width // LANES, rows, LANES), f32),
            pltpu.VMEM((rows + PAD, width), f32),
            pltpu.VMEM((rows, block), bf16),
            pltpu.VMEM((rows, block), bf16),
            small,
            pltpu.VMEM((nseq, PAD, width), f32),
            pltpu.VMEM((1, width), f32),
            small,
            small,
            dma, dma, dma((nseq - 1,)), dma((nseq,)),
        ],
        compiler_params=pltpu.CompilerParams(
            collective_id=2, has_side_effects=True, vmem_limit_bytes=VMEM_LIMIT
        ),
        name="rec_backward",
    )(gm, py, states, pxe, rate, ig, co, marks, gate_a, gate_i, vectors)


def on_device(
    ndp, nseq,
    tokens, doc_lengths, norm_gain, w_y, w_x, gate_a, gate_i, bias_a, bias_i, conv_w, conv_b,
    decay_param, w_out, mlp_gain, w_gate, w_up, w_down, cotangent,
):
    local_len, features = tokens.shape
    rows_here = w_y.shape[0]
    width_here = w_y.shape[1]
    hidden_here = w_gate.shape[1]
    block = gate_a.shape[1]
    bits = [1 << k for k in range(ndp.bit_length() - 1)]

    def inner(value):
        lead = value.shape[:-1]
        return jnp.swapaxes(value.reshape(*lead, ndp, nseq, rows_here), -3, -2).reshape(*lead, features)

    def outer(value):
        lead = value.shape[:-1]
        return jnp.swapaxes(value.reshape(*lead, nseq, ndp, rows_here), -3, -2).reshape(*lead, features)

    def gather(weight):
        return lax.all_gather(weight, ("seq", "dp"), axis=0, tiled=True)

    def spread(value):
        for bit in reversed(bits):
            value = jnp.concatenate([value, xor_permute(value, "dp", bit)], axis=0)
        return value

    def collect(value):
        for bit in bits:
            half = value.shape[0] // 2
            value = (value[:half] + xor_permute(value[half:], "dp", bit)).astype(bf16)
        return value.astype(f32) + xor_permute(value, "mp", 1).astype(f32)

    position = lax.axis_index("seq") * local_len + jnp.arange(local_len + PAD, dtype=jnp.int32)
    lengths_row = doc_lengths[0]
    starts = jnp.cumsum(lengths_row) - lengths_row
    resets = jnp.any(position[:, None] == starts[None, :], axis=1)
    doc_start = jnp.max(jnp.where(starts[None, :] <= position[:, None], starts[None, :], 0), axis=1)
    marks = jnp.stack(
        [1.0 - resets.astype(f32)] + [(position - lag >= doc_start).astype(f32) for lag in (1, 2, 3)]
    )
    marks = jnp.broadcast_to(marks[:, :, None], (4, local_len + PAD, block))
    vectors = jnp.concatenate(
        [conv_w, conv_b[None], bias_a[None], bias_i[None], jax.nn.softplus(-decay_param)[None]], axis=0
    )

    all_y, all_x = gather(w_y), gather(w_x)
    mlp_rows = lax.all_to_all(
        jnp.stack([w_gate, w_up, w_down]).reshape(3, rows_here, ndp, hidden_here // ndp),
        "dp", 2, 1, tiled=True,
    ).reshape(3, ndp * rows_here, hidden_here // ndp)
    all_out = gather(w_out)
    all_gate, all_up, all_down = (
        lax.all_gather(mlp_rows[k], "seq", axis=0, tiled=True) for k in range(3)
    )
    gain_one, gain_two = inner(norm_gain), inner(mlp_gain)
    resid = inner(tokens).astype(f32)
    scale_one = norm_scale(resid)
    acts_one = (resid * scale_one * gain_one).astype(bf16)
    pre_y, pre_x = matmul(acts_one, all_y), matmul(acts_one, all_x)
    mixed_rec, states, pxe, rate, ig, conv_out = rec_forward(
        nseq, pre_x, pre_y, marks, gate_a, gate_i, vectors
    )

    cot = inner(cotangent)
    per = local_len // CHUNKS
    pieces = []
    for k in range(CHUNKS):
        here = slice(k * per, (k + 1) * per)
        part = contract(mixed_rec[here], all_out).astype(bf16)
        middle = resid[here] + (part.astype(f32) + xor_permute(part, "mp", 1).astype(f32))
        scale_two = norm_scale(middle)
        acts = spread((middle * scale_two * gain_two).astype(bf16))
        cots = spread(cot[here])
        pre_gate, pre_up = matmul(acts, all_gate), matmul(acts, all_up)
        gelu, slope = gelu_parts(pre_gate)
        mixed = (gelu * pre_up).astype(bf16)
        grad_mixed = matmul(cots, all_down)
        grad_gate = (grad_mixed * pre_up * slope).astype(bf16)
        grad_up = (grad_mixed * gelu).astype(bf16)
        grad_acts = collect(
            (contract(grad_gate, all_gate) + contract(grad_up, all_up)).astype(bf16)
        )
        normed = middle * scale_two
        grad_normed = grad_acts * gain_two
        grad_middle = cot[here].astype(f32) + scale_two * (
            grad_normed - normed * jnp.mean(grad_normed * normed, axis=-1, keepdims=True)
        )
        gain_part = jnp.sum(grad_acts * normed, axis=0)
        final = middle + collect(contract(mixed, all_down).astype(bf16))
        pieces.append((acts, cots, mixed, grad_gate, grad_up, grad_middle, gain_part, final.astype(bf16)))
    acts, cots, mixed, grad_gate, grad_up, grad_middle, gain_parts, output = (
        [piece[j] for piece in pieces] for j in range(8)
    )
    join = functools.partial(jnp.concatenate, axis=0)
    acts, cots, mixed, grad_gate, grad_up = map(join, (acts, cots, mixed, grad_gate, grad_up))
    grad_middle = join(grad_middle)

    def reduce_mlp(left, right):
        total = lax.psum_scatter(
            contract_rows(left, right).astype(bf16), "seq", scatter_dimension=0, tiled=True
        )
        return total

    mlp_sums = jnp.stack(
        [reduce_mlp(acts, grad_gate), reduce_mlp(acts, grad_up), reduce_mlp(cots, mixed)]
    )
    mlp_sums = lax.all_to_all(mlp_sums, "dp", 1, 2, tiled=True).astype(f32)

    grad_middle_low = grad_middle.astype(bf16)
    grad_mixed_rec = matmul(grad_middle_low, all_out)
    grad_pre_y, grad_pre_x, grad_gate_a, grad_gate_i, sums = rec_backward(
        nseq, grad_mixed_rec, pre_y, states, pxe, rate, ig, conv_out, marks, gate_a, gate_i, vectors
    )
    part = (contract(grad_pre_y, all_y) + contract(grad_pre_x, all_x)).astype(bf16)
    grad_acts = part.astype(f32) + xor_permute(part, "mp", 1).astype(f32)
    normed = resid * scale_one
    grad_normed = grad_acts * gain_one
    input_grad = grad_middle + scale_one * (
        grad_normed - normed * jnp.mean(grad_normed * normed, axis=-1, keepdims=True)
    )

    def reduce_rec(left, right):
        return lax.psum_scatter(
            contract_rows(left, right).astype(bf16), ("seq", "dp"), scatter_dimension=0, tiled=True
        ).astype(f32)

    grad_w_out = reduce_rec(grad_middle_low, mixed_rec)
    grad_w_y = reduce_rec(acts_one, grad_pre_y)
    grad_w_x = reduce_rec(acts_one, grad_pre_x)
    totals = lax.psum(
        (
            grad_gate_a,
            grad_gate_i,
            sums,
            jnp.sum(grad_acts * normed, axis=0),
            functools.reduce(jnp.add, gain_parts),
        ),
        ("dp", "seq"),
    )
    sums = totals[2]
    return (
        outer(join(output)),
        outer(input_grad),
        outer(totals[3]),
        grad_w_y,
        grad_w_x,
        totals[0],
        totals[1],
        sums[0],
        sums[1],
        sums[4:8],
        sums[3],
        sums[2] * jax.nn.sigmoid(-decay_param),
        grad_w_out,
        outer(totals[4]),
        mlp_sums[0],
        mlp_sums[1],
        mlp_sums[2],
    )


def solution(mesh):
    rows, cols = P(("dp", "seq"), None), P(("dp", "seq"), "mp")
    return jax.shard_map(
        functools.partial(on_device, mesh.shape["dp"], mesh.shape["seq"]),
        mesh=mesh,
        in_specs=(
            rows, P("dp", None), P(), cols, cols, P("mp", None, None), P("mp", None, None), P("mp"), P("mp"),
            P(None, "mp"), P("mp"), P("mp"), cols, P(), cols, cols, cols, rows,
        ),
        out_specs=(
            rows, rows, P(), cols, cols, P("mp", None, None), P("mp", None, None), P("mp"), P("mp"),
            P(None, "mp"), P("mp"), P("mp"), cols, P(), cols, cols, cols,
        ),
        check_vma=False,
    )
```

```python
import functools

import jax
import jax.numpy as jnp
from jax import lax
from jax.experimental import pallas as pl
from jax.experimental.pallas import tpu as pltpu
from jax.sharding import PartitionSpec as P

epsilon = 1e-06
decay_scale = 8.0
MESH = pl.DeviceIdType.MESH
VMEM_LIMIT = 60 * 2**20
SEGMENTS = 8
PAD = 8
bf16 = jnp.bfloat16
f32 = jnp.float32


def xor_permute(value, axis, bit):
    count = lax.axis_size(axis)
    return lax.ppermute(value, axis, [(source, source ^ bit) for source in range(count)])


def matmul(left, right):
    return jnp.dot(left, right, preferred_element_type=f32)


def contract(left, right):
    return lax.dot_general(left, right, (((1,), (1,)), ((), ())), preferred_element_type=f32)


def contract_rows(left, right):
    return lax.dot_general(left, right, (((0,), (0,)), ((), ())), preferred_element_type=f32)


def norm_scale(values):
    return lax.rsqrt(jnp.mean(values * values, axis=-1, keepdims=True) + epsilon)


def gelu_parts(y):
    c = 0.7978845608028654
    u = c * (y + 0.044715 * y * y * y)
    t = jnp.tanh(u)
    half = 0.5 * (1.0 + t)
    slope = half + 0.5 * y * (1.0 - t * t) * (c * (1.0 + 3.0 * 0.044715 * y * y))
    return y * half, slope


def one_minus_square(log_decay, decay):
    y = -2.0 * log_decay
    series = 1.0 - y * (1.0 / 5.0)
    for k in (4, 3, 2):
        series = 1.0 - y * (1.0 / k) * series
    return jnp.where(y < 0.1, y * series, 1.0 - decay * decay)


def seq_barrier(nseq):
    dp, z, mp = (lax.axis_index(a) for a in ("dp", "seq", "mp"))
    barrier = pltpu.get_barrier_semaphore()
    for step in range(1, nseq):
        pl.semaphore_signal(
            barrier, inc=1, device_id=(dp, lax.rem(z + step, nseq), mp), device_id_type=MESH
        )
    pl.semaphore_wait(barrier, nseq - 1)


def to_seq(src, dst, send_sem, recv_sem, target):
    dp, mp = (lax.axis_index(a) for a in ("dp", "mp"))
    return pltpu.make_async_remote_copy(
        src_ref=src,
        dst_ref=dst,
        send_sem=send_sem,
        recv_sem=recv_sem,
        device_id=(dp, target, mp),
        device_id_type=MESH,
    )


LANES = 128


def spread_lanes(value, width):
    return jnp.concatenate([value] * (width // value.shape[1]), axis=1)


def rec_forward_kernel(
    nseq, heads, block,
    acts_ref, wx_ref, wy_ref, marks_ref, ga_ref, gi_ref, vec_ref,
    mixed_ref, states_out, pxe_out, py_out, rate_out, ig_out, co_out,
    wy_s, states_s, pxe_s, py_s, rate_s, ig_s, co_s,
    a_s, b_s, tail_s, msg, got, state_in, halo, load_sem, store_sems, halo_send, halo_recv, end_send, end_recv,
):
    rows, width = mixed_ref.shape
    seg = rows // SEGMENTS
    z = lax.axis_index("seq")
    load = pltpu.make_async_copy(wy_ref, wy_s, load_sem)
    load.start()
    seq_barrier(nseq)

    def store(k, source, target):
        return pltpu.make_async_copy(source, target, store_sems.at[k])

    pairs = (
        (py_s, py_out), (pxe_s, pxe_out), (rate_s, rate_out), (ig_s, ig_out), (co_s, co_out), (states_s, states_out),
    )

    def block_cols(h):
        return pl.ds(pl.multiple_of(h * block, block), block)

    def project_x(h, _):
        product = matmul(acts_ref[...], wx_ref[:, block_cols(h)])
        pxe_s[pl.ds(PAD, rows), block_cols(h)] = product.astype(bf16).astype(f32)
        return 0

    lax.fori_loop(0, heads, project_x, 0)
    tail_s[...] = pxe_s[pl.ds(rows, PAD), :]

    def halo_copy(target):
        return to_seq(tail_s, halo, halo_send, halo_recv, target)

    @pl.when(z < nseq - 1)
    def _():
        halo_copy(z + 1).start()

    load.wait()

    def project_y(h, _):
        py_s[:, block_cols(h)] = matmul(acts_ref[...], wy_s[:, block_cols(h)])
        return 0

    lax.fori_loop(0, heads, project_y, 0)
    store(0, *pairs[0]).start()

    @pl.when(z == 0)
    def _():
        halo[...] = jnp.zeros_like(halo)

    @pl.when(z > 0)
    def _():
        halo_copy(z).wait_recv()

    pxe_s[pl.ds(0, PAD), :] = halo[...]
    store(1, *pairs[1]).start()

    def head(h, _):
        cols = block_cols(h)

        def part(r, _):
            at = pl.ds(pl.multiple_of(r * seg, seg), seg)
            window = pxe_s[pl.ds(pl.multiple_of(r * seg, seg), seg + PAD), cols]
            conv_out = vec_ref[4:5, cols] + vec_ref[0:1, cols] * window[PAD:]
            for lag in (1, 2, 3):
                shifted = pltpu.roll(window, lag, 0)[PAD:]
                conv_out = conv_out + vec_ref[lag : lag + 1, cols] * shifted * spread_lanes(marks_ref[lag, at, :], block)
            low = conv_out.astype(bf16)
            gate_r = matmul(low, ga_ref[h])
            gate_x = matmul(low, gi_ref[h])
            rate = jax.nn.sigmoid(gate_r + vec_ref[5:6, cols])
            ig = jax.nn.sigmoid(gate_x + vec_ref[6:7, cols])
            log_decay = -decay_scale * rate * vec_ref[7:8, cols]
            decay = jnp.exp(log_decay)
            mult = jnp.sqrt(one_minus_square(log_decay, decay))
            a_s[at, cols] = decay * spread_lanes(marks_ref[0, at, :], block)
            b_s[at, cols] = conv_out * ig * mult
            rate_s[at, cols] = rate
            ig_s[at, cols] = ig
            co_s[at, cols] = conv_out
            return 0

        lax.fori_loop(0, SEGMENTS, part, 0)
        return 0

    lax.fori_loop(0, heads, head, 0)
    for k in (2, 3, 4):
        store(k, *pairs[k]).start()
    row = lax.broadcasted_iota(jnp.int32, (8, width), 0)

    def turn(t, kept):
        prefix, state = kept
        at = pl.ds(pl.multiple_of(t * 8, 8), 8)
        decay, drive = a_s[at, :], b_s[at, :]
        for k in (1, 2, 4):
            inside = row >= k
            drive = decay * jnp.where(inside, pltpu.roll(drive, k, 0), 0.0) + drive
            decay = decay * jnp.where(inside, pltpu.roll(decay, k, 0), 1.0)
        drive = decay * state + drive
        decay = decay * prefix
        a_s[at, :] = decay
        b_s[at, :] = drive
        return decay[7:8], drive[7:8]

    one, zero = jnp.ones((1, width), f32), jnp.zeros((1, width), f32)
    prefix, state = lax.fori_loop(0, rows // 8, turn, (one, zero))
    msg[0:1, :] = prefix
    msg[1:2, :] = state
    msg[2:PAD, :] = jnp.zeros((PAD - 2, width), f32)
    for step in range(1, nseq):

        @pl.when(z + step < nseq)
        def _():
            to_seq(msg, got.at[z], end_send.at[step - 1], end_recv.at[z], z + step).start()

    state_in[...] = jnp.zeros_like(state_in)
    for source in range(nseq - 1):

        @pl.when(source < z)
        def _():
            to_seq(msg, got.at[source], end_send.at[0], end_recv.at[source], z).wait_recv()
            state_in[...] = got[source, 0:1, :] * state_in[...] + got[source, 1:2, :]

    states_s[pl.ds(0, PAD), :] = jnp.broadcast_to(state_in[...], (PAD, width))

    def finish(i, _):
        s, h = i // heads, lax.rem(i, heads)
        cols = block_cols(h)
        at = pl.ds(pl.multiple_of(s * seg, seg), seg)
        states = b_s[at, cols] + a_s[at, cols] * state_in[:, cols]
        states_s[pl.ds(pl.multiple_of(PAD + s * seg, PAD), seg), cols] = states
        mixed_ref[at, cols] = (states * gelu_parts(py_s[at, cols])[0]).astype(bf16)
        return 0

    lax.fori_loop(0, SEGMENTS * heads, finish, 0)
    store(5, *pairs[5]).start()

    @pl.when(z < nseq - 1)
    def _():
        halo_copy(z).wait_send()

    for step in range(1, nseq):

        @pl.when(z + step < nseq)
        def _():
            to_seq(msg, got.at[z], end_send.at[step - 1], end_recv.at[z], z).wait_send()

    for k, pair in enumerate(pairs):
        store(k, *pair).wait()


def rec_forward(nseq, acts, all_x, all_y, marks, gate_a, gate_i, vectors):
    rows, width = acts.shape[0], all_x.shape[1]
    heads, block = gate_a.shape[:2]
    vmem, anywhere = pl.BlockSpec(memory_space=pltpu.VMEM), pl.BlockSpec(memory_space=pl.ANY)
    big, ext = (rows, width), (rows + PAD, width)
    kept = (ext, ext, big, big, big, big)
    small = pltpu.VMEM((PAD, width), f32)
    dma = pltpu.SemaphoreType.DMA
    return pl.pallas_call(
        functools.partial(rec_forward_kernel, nseq, heads, block),
        out_shape=[jax.ShapeDtypeStruct(big, bf16)] + [jax.ShapeDtypeStruct(shape, f32) for shape in kept],
        in_specs=[vmem, vmem, anywhere] + [vmem] * 4,
        out_specs=[vmem] + [anywhere] * 6,
        scratch_shapes=[
            pltpu.VMEM(all_y.shape, bf16),
            *[pltpu.VMEM(shape, f32) for shape in kept],
            pltpu.VMEM(big, f32),
            pltpu.VMEM(big, f32),
            small,
            small,
            pltpu.VMEM((nseq, PAD, width), f32),
            pltpu.VMEM((1, width), f32),
            small,
            dma, dma((6,)), dma, dma, dma((nseq - 1,)), dma((nseq,)),
        ],
        compiler_params=pltpu.CompilerParams(
            collective_id=1, has_side_effects=True, vmem_limit_bytes=VMEM_LIMIT
        ),
        cost_estimate=cost(35),
        name="rec_forward",
    )(acts, all_x, all_y, marks, gate_a, gate_i, vectors)


def rec_backward_kernel(
    nseq, heads, block,
    low_ref, out_ref, marks_ref, ga_ref, gi_ref, vec_ref, py_ref, states_ref, rate_ref, pxe_ref, ig_ref, co_ref,
    gpy_ref, gpx_ref, gga_ref, ggi_ref, sums_ref,
    py_s, states_s, rate_s, pxe_s, ig_s, co_s, w_s, b_s, g_s, gm_s, gc_s, gr_s, gx_s,
    msg, got, grad_in, head_s, load_sems, halo_send, halo_recv, end_send, end_recv,
):
    rows, width = gpy_ref.shape
    seg = rows // SEGMENTS
    z = lax.axis_index("seq")
    loads = [
        pltpu.make_async_copy(source, target, load_sems.at[k])
        for k, (source, target) in enumerate(
            ((py_ref, py_s), (states_ref, states_s), (rate_ref, rate_s), (pxe_ref, pxe_s), (ig_ref, ig_s), (co_ref, co_s))
        )
    ]
    for load in loads:
        load.start()
    seq_barrier(nseq)
    for load in loads[:3]:
        load.wait()

    def block_cols(h):
        return pl.ds(pl.multiple_of(h * block, block), block)

    def first(h, _):
        cols = block_cols(h)
        gm_s[...] = matmul(low_ref[...], out_ref[:, cols])

        def part(s, _):
            at = pl.ds(pl.multiple_of(s * seg, seg), seg)
            gelu, slope = gelu_parts(py_s[at, cols])
            gm = gm_s[at, :]
            states = states_s[pl.ds(pl.multiple_of(PAD + s * seg, PAD), seg), cols]
            gpy_ref[at, cols] = (gm * states * slope).astype(bf16)
            decay = jnp.exp(-decay_scale * rate_s[at, cols] * vec_ref[7:8, cols])
            decay = decay * spread_lanes(marks_ref[0, at, :], block)
            grad = gm * gelu
            b_s[at, cols] = grad
            w_s[at, cols] = decay
            g_s[at, cols] = grad * decay
            return 0

        lax.fori_loop(0, SEGMENTS, part, 0)
        return 0

    lax.fori_loop(0, heads, first, 0)
    row = lax.broadcasted_iota(jnp.int32, (8, width), 0)

    def turn(i, kept):
        suffix, owed = kept
        at = pl.ds(pl.multiple_of(rows - 8 - i * 8, 8), 8)
        decay, grad = w_s[at, :], g_s[at, :]
        for k in (1, 2, 4):
            inside = row < 8 - k
            grad = decay * jnp.where(inside, pltpu.roll(grad, 8 - k, 0), 0.0) + grad
            decay = decay * jnp.where(inside, pltpu.roll(decay, 8 - k, 0), 1.0)
        grad = decay * owed + grad
        decay = decay * suffix
        w_s[at, :] = decay
        g_s[at, :] = grad
        return decay[0:1], grad[0:1]

    one, zero = jnp.ones((1, width), f32), jnp.zeros((1, width), f32)
    suffix, owed = lax.fori_loop(0, rows // 8, turn, (one, zero))
    w_s[pl.ds(rows, PAD), :] = jnp.ones((PAD, width), f32)
    g_s[pl.ds(rows, PAD), :] = jnp.zeros((PAD, width), f32)
    msg[0:1, :] = suffix
    msg[1:2, :] = owed
    msg[2:PAD, :] = jnp.zeros((PAD - 2, width), f32)
    for step in range(1, nseq):

        @pl.when(z >= step)
        def _():
            to_seq(msg, got.at[z], end_send.at[step - 1], end_recv.at[z], z - step).start()

    for load in loads[3:]:
        load.wait()
    grad_in[...] = jnp.zeros_like(grad_in)
    for source in range(nseq - 1, 0, -1):

        @pl.when(source > z)
        def _():
            to_seq(msg, got.at[source], end_send.at[0], end_recv.at[source], z).wait_recv()
            grad_in[...] = got[source, 0:1, :] * grad_in[...] + got[source, 1:2, :]

    def fold(value):
        return jnp.sum(value.reshape(seg // 8, 8, block), axis=0)

    def head(h, _):
        cols = block_cols(h)
        shrink = vec_ref[7:8, cols]

        def part(s, sums):
            at = pl.ds(pl.multiple_of(s * seg, seg), seg)
            ahead = pl.ds(pl.multiple_of(s * seg, seg), seg + PAD)
            owed = g_s[ahead, cols] + w_s[ahead, cols] * grad_in[:, cols]
            carry = b_s[at, cols] + pltpu.roll(owed, seg + PAD - 1, 0)[:seg]
            before = pltpu.roll(states_s[ahead, cols], 1, 0)[PAD:]
            rate, ig, conv_out = rate_s[at, cols], ig_s[at, cols], co_s[at, cols]
            log_decay = -decay_scale * rate * shrink
            decay = jnp.exp(log_decay)
            square = one_minus_square(log_decay, decay)
            inverse = lax.rsqrt(square)
            gated = carry * ig
            direct = gated * (square * inverse)
            gated = gated * conv_out
            keep = spread_lanes(marks_ref[0, at, :], block)
            grad_log = carry * before * decay * keep - gated * (decay * decay) * inverse
            spread = grad_log * decay_scale * rate
            grad_r = -spread * shrink * (1.0 - rate)
            grad_x = direct * conv_out * (1.0 - ig)
            low_r, low_x = grad_r.astype(bf16), grad_x.astype(bf16)
            gr_s[at, :] = low_r
            gx_s[at, :] = low_x
            grad_conv = direct + contract(low_r, ga_ref[h]) + contract(low_x, gi_ref[h])
            gc_s[at, cols] = grad_conv
            window = pxe_s[ahead, cols]
            terms = [grad_r, grad_x, spread, grad_conv, grad_conv * window[PAD:]]
            for lag in (1, 2, 3):
                terms.append(grad_conv * spread_lanes(marks_ref[lag, at, :], block) * pltpu.roll(window, lag, 0)[PAD:])
            return tuple(total + fold(term) for total, term in zip(sums, terms))

        sums = lax.fori_loop(
            0, SEGMENTS, part, tuple(jnp.zeros((8, block), f32) for _ in range(8))
        )
        for k, total in enumerate(sums):
            sums_ref[k : k + 1, cols] = jnp.sum(total, axis=0, keepdims=True)
        low = co_s[:, cols].astype(bf16)
        gga_ref[h] = contract_rows(low, gr_s[...])
        ggi_ref[h] = contract_rows(low, gx_s[...])
        return 0

    lax.fori_loop(0, heads, head, 0)
    head_s[...] = gc_s[pl.ds(0, PAD), :]

    @pl.when(z > 0)
    def _():
        to_seq(head_s, gc_s.at[pl.ds(rows, PAD)], halo_send, halo_recv, z - 1).start()

    @pl.when(z < nseq - 1)
    def _():
        to_seq(head_s, gc_s.at[pl.ds(rows, PAD)], halo_send, halo_recv, z).wait_recv()

    @pl.when(z == nseq - 1)
    def _():
        gc_s[pl.ds(rows, PAD), :] = jnp.zeros((PAD, width), f32)

    def final(i, _):
        s, h = i // heads, lax.rem(i, heads)
        cols = block_cols(h)
        at = pl.ds(pl.multiple_of(s * seg, seg), seg)
        ahead = pl.ds(pl.multiple_of(s * seg, seg), seg + PAD)
        owed = gc_s[ahead, cols]
        grad = vec_ref[0:1, cols] * owed[:seg]
        for lag in (1, 2, 3):
            shifted = owed * spread_lanes(marks_ref[lag, ahead, :], block)
            shifted = pltpu.roll(shifted, seg + PAD - lag, 0)[:seg]
            grad = grad + vec_ref[lag : lag + 1, cols] * shifted
        gpx_ref[at, cols] = grad.astype(bf16)
        return 0

    lax.fori_loop(0, SEGMENTS * heads, final, 0)

    @pl.when(z > 0)
    def _():
        to_seq(head_s, gc_s.at[pl.ds(rows, PAD)], halo_send, halo_recv, z).wait_send()

    for step in range(1, nseq):

        @pl.when(z >= step)
        def _():
            to_seq(msg, got.at[z], end_send.at[step - 1], end_recv.at[z], z).wait_send()


def rec_backward(nseq, low, all_out, marks, gate_a, gate_i, vectors, kept):
    rows, width = low.shape[0], all_out.shape[1]
    heads, block = gate_a.shape[:2]
    vmem, anywhere = pl.BlockSpec(memory_space=pltpu.VMEM), pl.BlockSpec(memory_space=pl.ANY)
    grads = jax.ShapeDtypeStruct((rows, width), bf16)
    gates = jax.ShapeDtypeStruct(gate_a.shape, f32)
    small = pltpu.VMEM((PAD, width), f32)
    ext = pltpu.VMEM((rows + PAD, width), f32)
    dma = pltpu.SemaphoreType.DMA
    return pl.pallas_call(
        functools.partial(rec_backward_kernel, nseq, heads, block),
        out_shape=(grads, grads, gates, gates, jax.ShapeDtypeStruct((8, width), f32)),
        in_specs=[vmem] * 6 + [anywhere] * len(kept),
        out_specs=[vmem] * 5,
        scratch_shapes=[
            *[pltpu.VMEM(k.shape, k.dtype) for k in kept],
            ext,
            pltpu.VMEM((rows, width), f32),
            ext,
            pltpu.VMEM((rows, block), f32),
            ext,
            pltpu.VMEM((rows, block), bf16),
            pltpu.VMEM((rows, block), bf16),
            small,
            pltpu.VMEM((nseq, PAD, width), f32),
            pltpu.VMEM((1, width), f32),
            small,
            dma((len(kept),)), dma, dma, dma((nseq - 1,)), dma((nseq,)),
        ],
        compiler_params=pltpu.CompilerParams(
            collective_id=2, has_side_effects=True, vmem_limit_bytes=VMEM_LIMIT
        ),
        cost_estimate=cost(45),
        name="rec_backward",
    )(low, all_out, marks, gate_a, gate_i, vectors, *kept)


def flip(index, mask):
    bit = 1
    while bit <= mask:
        if mask & bit:
            index = index + bit - 2 * bit * lax.rem(index // bit, 2)
        bit *= 2
    return index


def neighbour_barrier(ndp, nseq):
    dp, z, mp = (lax.axis_index(a) for a in ("dp", "seq", "mp"))
    barrier = pltpu.get_barrier_semaphore()

    def greet(target):
        pl.semaphore_signal(barrier, inc=1, device_id=target, device_id_type=MESH)

    for mask in range(1, ndp):
        greet((flip(dp, mask), z, mp))

    @pl.when(z > 0)
    def _():
        greet((dp, z - 1, mp))

    @pl.when(z < nseq - 1)
    def _():
        greet((dp, z + 1, mp))

    neighbours = lax.div(z + nseq - 1, nseq) + lax.div(2 * nseq - 2 - z, nseq)
    pl.semaphore_wait(barrier, ndp - 1 + neighbours)


class Copies:
    def __init__(self):
        self.sent = []

    def start(self, here, make):
        if here is None:
            make().start()
        else:

            @pl.when(here)
            def _():
                make().start()

        self.sent.append((here, make))

    def finish(self):
        for here, make in self.sent:
            if here is None:
                make().wait_send()
            else:

                @pl.when(here)
                def _():
                    make().wait_send()


def gather_kernel(ndp, nseq, side_first, split, *refs):
    count = len(side_first)
    shards, wide = refs[:count], refs[count : count + split]
    wholes, pieces = refs[count + split : 2 * count + split], refs[2 * count + split : 2 * (count + split)]
    local_sem, send, recv, piece_send, piece_recv = refs[2 * (count + split) :]
    dp, z, mp = (lax.axis_index(a) for a in ("dp", "seq", "mp"))
    rows = shards[0].shape[0]
    piece_cols = pieces[0].shape[1] if split else 0
    bits = [1 << k for k in range(1, ndp.bit_length() - 1)][::-1]
    copies = Copies()

    def valid(step):
        if step == 0:
            return None
        return z + step < nseq if step > 0 else z + step >= 0

    def copy(i, step, mask, there, mask_there, target):
        at = pl.ds(pl.multiple_of((flip(dp, mask) * nseq + z + step) * rows, rows), rows)
        index = (i, there + nseq - 1, mask_there)
        return pltpu.make_async_remote_copy(
            src_ref=shards[i] if step == 0 and mask == 0 and target is not None else wholes[i].at[at],
            dst_ref=wholes[i].at[at],
            send_sem=send.at[index],
            recv_sem=recv.at[index],
            device_id=(dp, z, mp) if target is None else target,
            device_id_type=MESH,
        )

    def along(i, step, mask):
        for way in (1, -1):
            if step * way > 0:
                continue
            near = z < nseq - 1 if way > 0 else z > 0
            here = near if step == 0 else near & valid(step)
            copies.start(
                here,
                functools.partial(copy, i, step, mask, step - way, mask, (dp, z + way, mp)),
            )

    def across(i, step, mask, bit):
        copies.start(
            valid(step),
            functools.partial(copy, i, step, mask, step, mask | bit, (flip(dp, bit), z, mp)),
        )

    def go_on(i, step, mask):
        if mask & 1:
            return
        lowest = mask & -mask if mask else ndp
        if side_first[i]:
            if step == 0:
                for bit in bits:
                    if bit < lowest:
                        across(i, step, mask, bit)
            along(i, step, mask)
        else:
            if mask == 0:
                along(i, step, mask)
            for bit in bits:
                if bit < lowest:
                    across(i, step, mask, bit)
        across(i, step, mask, 1)

    def arrive(i, step, mask):
        def wait():
            copy(i, step, mask, step, mask, None).wait_recv()

        if step == 0:
            wait()
        else:
            pl.when(valid(step))(wait)
        go_on(i, step, mask)

    def piece_copy(k, mask):
        cols = pl.ds(pl.multiple_of(flip(dp, mask) * piece_cols, LANES), piece_cols)
        src = wide[k].at[:, cols] if len(wide[k].shape) == 2 else wide[k].at[flip(dp, mask)]
        dst = pieces[k].at[pl.ds(pl.multiple_of(dp * rows, rows), rows)]
        if mask == 0:
            return pltpu.make_async_copy(src, dst, local_sem.at[count + k])
        return pltpu.make_async_remote_copy(
            src_ref=src, dst_ref=dst, send_sem=piece_send.at[k, mask], recv_sem=piece_recv.at[k, mask],
            device_id=(flip(dp, mask), z, mp), device_id_type=MESH,
        )

    def piece_arrived(k, mask):
        at = pl.ds(pl.multiple_of(flip(dp, mask) * rows, rows), rows)
        pltpu.make_async_remote_copy(
            src_ref=pieces[k].at[at], dst_ref=pieces[k].at[at], send_sem=piece_send.at[k, mask],
            recv_sem=piece_recv.at[k, mask], device_id=(dp, z, mp), device_id_type=MESH,
        ).wait_recv()

    neighbour_barrier(ndp, nseq)
    for i in range(count):
        here = pl.ds(pl.multiple_of((dp * nseq + z) * rows, rows), rows)
        pltpu.make_async_copy(shards[i], wholes[i].at[here], local_sem.at[i]).start()
    order = sorted(range(count), key=lambda i: not side_first[i])
    for i in order:
        go_on(i, 0, 0)
    masks = [0]
    for bit in bits:
        masks += [m | bit for m in masks]
    sides = masks[1:]
    first, last = [i for i in order if side_first[i]], [i for i in order if not side_first[i]]
    for i in first:
        for mask in sides:
            arrive(i, 0, mask)
    pieces_left = list(range(split))
    for step in range(1, nseq):
        if pieces_left:
            k = pieces_left.pop(0)
            for mask in range(ndp):
                piece_copy(k, mask).start()
        for i in order:
            arrive(i, -step, 0)
            arrive(i, step, 0)
        for i in last:
            for mask in sides:
                arrive(i, 1 - step, mask)
                if step > 1:
                    arrive(i, step - 1, mask)
        for i in first:
            for mask in sides:
                arrive(i, -step, mask)
                arrive(i, step, mask)
    for k in pieces_left:
        for mask in range(ndp):
            piece_copy(k, mask).start()
    for i in last:
        for mask in sides:
            arrive(i, 1 - nseq, mask)
            arrive(i, nseq - 1, mask)
    for i in range(count):
        for mask in masks:
            for step in range(1 - nseq, nseq):
                arrive(i, step, mask | 1)
    for k in range(split):
        for mask in range(1, ndp):
            piece_arrived(k, mask)
    for i in range(count):
        here = pl.ds(pl.multiple_of((dp * nseq + z) * rows, rows), rows)
        pltpu.make_async_copy(shards[i], wholes[i].at[here], local_sem.at[i]).wait()
    for k in range(split):
        piece_copy(k, 0).wait()
        for mask in range(1, ndp):
            piece_copy(k, mask).wait_send()
    copies.finish()


def gather_weights(ndp, nseq, shards, side_first, wide, number):
    rows = shards[0].shape[0]
    count, split = len(shards), len(wide)
    piece = wide[0].shape[1] // ndp if split else LANES
    if piece % LANES:
        wide = [jnp.swapaxes(w.reshape(rows, ndp, piece), 0, 1) for w in wide]
    dma = pltpu.SemaphoreType.DMA
    anywhere = pl.BlockSpec(memory_space=pl.ANY)
    return pl.pallas_call(
        functools.partial(gather_kernel, ndp, nseq, side_first, split),
        out_shape=[jax.ShapeDtypeStruct((ndp * nseq * rows, s.shape[1]), s.dtype) for s in shards]
        + [jax.ShapeDtypeStruct((ndp * rows, piece), w.dtype) for w in wide],
        in_specs=[anywhere] * (count + split),
        out_specs=[anywhere] * (count + split),
        scratch_shapes=[
            dma((count + split,)), dma((count, 2 * nseq - 1, ndp)), dma((count, 2 * nseq - 1, ndp)),
            dma((max(split, 1), ndp)), dma((max(split, 1), ndp)),
        ],
        compiler_params=pltpu.CompilerParams(collective_id=number, has_side_effects=True),
        name="gather_weights",
    )(*shards, *wide)


def reduce_kernel(ndp, nseq, kinds, *refs):
    lefts = max(kind[0] for kind in kinds if kind[0] is not None) + 1
    left_refs, refs = refs[:lefts], refs[lefts:]
    count = len(kinds)
    rights, outs = refs[:count], refs[count : 2 * count]
    buffers, refs = refs[2 * count : 9 * count], refs[9 * count :]
    core_out, core_in, side_out, side_in, flow_out, up_in, down_in = (
        buffers[k * count : (k + 1) * count] for k in range(7)
    )
    acc, core_sems, side_sems, flow_sems, up_sems, down_sems = refs
    dp, z, mp = (lax.axis_index(a) for a in ("dp", "seq", "mp"))
    evens = list(range(0, ndp, 2))
    bits = [1 << k for k in range(1, ndp.bit_length() - 1)][::-1]
    order = [s for k in range(nseq - 1, 0, -1) for s in (k, -k)] + [0]
    copies = Copies()
    me = (dp, z, mp)

    def valid(step):
        if step == 0:
            return None
        return z + step < nseq if step > 0 else z + step >= 0

    def under(here, body):
        if here is None:
            body()
        else:
            pl.when(here)(body)

    def remote(src, dst, send_sem, recv_sem, target):
        return pltpu.make_async_remote_copy(
            src_ref=src, dst_ref=dst, send_sem=send_sem, recv_sem=recv_sem,
            device_id=target, device_id_type=MESH,
        )

    def core(i, step, mask):
        at = (z + step, mask // 2)
        return remote(
            core_out[i].at[at], core_in[i].at[at], core_sems.at[(0, i, *at)], core_sems.at[(1, i, *at)],
            (flip(dp, 1), z, mp),
        )

    def side(i, step, mask, bit):
        at = (z + step, mask // 2 - 1)
        return remote(
            side_out[i].at[at], side_in[i].at[at], side_sems.at[(0, i, *at)], side_sems.at[(1, i, *at)],
            (flip(dp, bit), z, mp),
        )

    def flow(i, step, way):
        into, sems = (up_in, up_sems) if way > 0 else (down_in, down_sems)
        return remote(
            flow_out[i].at[z + step], into[i].at[z + step], flow_sems.at[i, z + step], sems.at[i, z + step],
            (dp, z + way, mp),
        )

    def product(i, step, mask):
        rows = kinds[i][2]
        start = pl.multiple_of((flip(dp, mask) * nseq + z + step) * rows, rows)
        left = kinds[i][0]
        if left is None:
            return rights[i][pl.ds(start, rows), :]
        return jnp.dot(left_refs[left][pl.ds(start, rows), :], rights[i][...], preferred_element_type=f32)

    def block(ref, i, step, *more):
        return ref[i][(z + step, *more)].astype(f32)

    def store(ref, value, i, step, *more):
        ref[i][(z + step, *more)] = value.astype(bf16)

    neighbour_barrier(ndp, nseq)
    for i in range(count):
        for step in order:

            def to_core():
                for mask in evens:
                    store(core_out, product(i, step, mask | 1), i, step, mask // 2)

            under(valid(step), to_core)
            for mask in evens:
                copies.start(valid(step), functools.partial(core, i, step, mask))
    for i in range(count):
        for step in order:
            for mask in evens[:0:-1]:
                bit = 1 << (mask.bit_length() - 1)

                def to_side():
                    core(i, step, mask).wait_recv()
                    total = product(i, step, mask) + block(core_in, i, step, mask // 2)
                    for more in bits:
                        if more > bit:
                            side(i, step, mask | more, more).wait_recv()
                            total = total + block(side_in, i, step, (mask | more) // 2 - 1)
                    store(side_out, total, i, step, mask // 2 - 1)

                under(valid(step), to_side)
                copies.start(valid(step), functools.partial(side, i, step, mask, bit))
    for i in range(count):
        spot = (pl.ds(0, kinds[i][2]), pl.ds(0, kinds[i][1]))
        for step in order:

            def to_flow():
                core(i, step, 0).wait_recv()
                acc[spot] = product(i, step, 0) + block(core_in, i, step, 0)
                for more in bits:
                    side(i, step, more, more).wait_recv()
                    acc[spot] += block(side_in, i, step, more // 2 - 1)

                def add(into, way):
                    flow(i, step, way).wait_recv()
                    acc[spot] += block(into, i, step)

                if step >= 0:
                    pl.when(z > 0)(lambda: add(up_in, 1))
                if step <= 0:
                    pl.when(z < nseq - 1)(lambda: add(down_in, -1))
                if step:
                    store(flow_out, acc[spot], i, step)
                else:
                    outs[i][...] = acc[spot]

            under(valid(step), to_flow)
            if step:
                copies.start(valid(step), functools.partial(flow, i, step, 1 if step > 0 else -1))
    copies.finish()


def reduce_weights(ndp, nseq, lefts, rights, number):
    blocks = ndp * nseq
    kinds = [(k, r.shape[1], (r if k is None else lefts[k].T).shape[0] // blocks) for k, r in rights]
    count, evens = len(rights), ndp // 2
    vmem = pl.BlockSpec(memory_space=pltpu.VMEM)
    dma = pltpu.SemaphoreType.DMA
    low = functools.partial(pltpu.VMEM, dtype=bf16)

    def buffers(*lead):
        return [low((nseq, *lead, rows, width)) for _, width, rows in kinds]

    return pl.pallas_call(
        functools.partial(reduce_kernel, ndp, nseq, kinds),
        out_shape=[jax.ShapeDtypeStruct((rows, width), f32) for _, width, rows in kinds],
        in_specs=[vmem] * (len(lefts) + count),
        out_specs=[vmem] * count,
        scratch_shapes=[
            *buffers(evens), *buffers(evens), *buffers(evens - 1), *buffers(evens - 1),
            *buffers(), *buffers(), *buffers(),
            pltpu.VMEM((max(kind[2] for kind in kinds), max(kind[1] for kind in kinds)), f32),
            dma((2, count, nseq, evens)), dma((2, count, nseq, evens)),
            dma((count, nseq)), dma((count, nseq)), dma((count, nseq)),
        ],
        compiler_params=pltpu.CompilerParams(
            collective_id=number, has_side_effects=True, vmem_limit_bytes=VMEM_LIMIT
        ),
        cost_estimate=cost(100),
        name="reduce_weights",
    )(*[left.T for left in lefts], *[r for _, r in rights])


PART = 64


def cost(us):
    return pl.CostEstimate(flops=int(us * 1e9), bytes_accessed=int(us * 1e5), transcendentals=0)


def peers_barrier(ndp):
    dp, z, mp = (lax.axis_index(a) for a in ("dp", "seq", "mp"))
    barrier = pltpu.get_barrier_semaphore()
    for mask in range(1, ndp):
        pl.semaphore_signal(barrier, inc=1, device_id=(flip(dp, mask), z, mp), device_id_type=MESH)
    pl.semaphore_signal(barrier, inc=1, device_id=(dp, z, 1 - mp), device_id_type=MESH)
    pl.semaphore_wait(barrier, ndp)


def doubling(ndp):
    bits = [1 << k for k in range(1, ndp.bit_length() - 1)][::-1]
    masks = [0]
    for bit in bits:
        masks += [mask | bit for mask in masks]
    return bits, masks


def enter_kernel(
    ndp, mixed_ref, out_ref, tokens_ref, gain_ref, *refs
):
    bits, masks = doubling(ndp)
    cots, refs = refs[: len(masks)], refs[len(masks) :]
    middle_ref, acts_ref, all_cots = refs[:3]
    mine, theirs, normed, mine_sem, theirs_sem, own_sem, send, recv, cot_own, cot_send, cot_recv = refs[3:]
    rows = mixed_ref.shape[0]
    parts = rows // PART
    dp, z, mp = (lax.axis_index(a) for a in ("dp", "seq", "mp"))
    peers_barrier(ndp)

    def at(c):
        return pl.ds(pl.multiple_of(c * PART, PART), PART)

    def exchange(c):
        return pltpu.make_async_remote_copy(
            src_ref=mine.at[at(c)], dst_ref=theirs.at[at(c)], send_sem=mine_sem.at[c], recv_sem=theirs_sem.at[c],
            device_id=(dp, z, 1 - mp), device_id_type=MESH,
        )

    def hand(c, mask, bit):
        return pltpu.make_async_remote_copy(
            src_ref=acts_ref.at[mask, at(c)] if mask else normed.at[at(c)],
            dst_ref=acts_ref.at[mask | bit, at(c)],
            send_sem=send.at[mask | bit, c],
            recv_sem=recv.at[mask | bit, c],
            device_id=(flip(dp, bit), z, mp),
            device_id_type=MESH,
        )

    def own(c):
        return pltpu.make_async_copy(normed.at[at(c)], acts_ref.at[0, at(c)], own_sem.at[c])

    def cot_copy(k):
        return pltpu.make_async_copy(cots[k], all_cots.at[masks[k]], cot_own.at[k])

    def cot_hand(k):
        return pltpu.make_async_remote_copy(
            src_ref=cots[k], dst_ref=all_cots.at[masks[k] | 1], send_sem=cot_send.at[k], recv_sem=cot_recv.at[k],
            device_id=(flip(dp, 1), z, mp), device_id_type=MESH,
        )

    def project(k, _):
        several = pl.ds(pl.multiple_of(k * 4 * PART, 4 * PART), 4 * PART)
        mine[several, :] = contract(mixed_ref[several, :], out_ref[...]).astype(bf16)
        for c in range(4):
            exchange(4 * k + c).start()
        return 0

    lax.fori_loop(0, parts // 4, project, 0)
    for k in range(len(masks)):
        cot_copy(k).start()
        cot_hand(k).start()

    def norm(c, _):
        exchange(c).wait_recv()
        both = mine[at(c), :].astype(f32) + theirs[at(c), :].astype(f32)
        middle = tokens_ref[at(c), :].astype(f32) + both
        middle_ref[at(c), :] = middle
        scale = lax.rsqrt(jnp.mean(middle * middle, axis=-1, keepdims=True) + epsilon)
        normed[at(c), :] = (middle * scale * gain_ref[...]).astype(bf16)
        own(c).start()
        for bit in bits + [1]:
            hand(c, 0, bit).start()
        return 0

    lax.fori_loop(0, parts, norm, 0)
    for mask in masks[1:]:

        def pass_on(c, _):
            hand(c, mask & (mask - 1), mask & -mask).wait_recv()
            for bit in bits + [1]:
                if bit < mask & -mask:
                    hand(c, mask, bit).start()
            return 0

        lax.fori_loop(0, parts, pass_on, 0)

    def finish(c, _):
        own(c).wait()
        exchange(c).wait_send()
        for mask in masks:
            hand(c, mask, 1).wait_recv()
            for bit in bits + [1]:
                if mask == 0 or bit < mask & -mask:
                    hand(c, mask, bit).wait_send()
        return 0

    lax.fori_loop(0, parts, finish, 0)
    for k in range(len(masks)):
        cot_copy(k).wait()
        cot_hand(k).wait()


def enter_mlp(ndp, mixed, all_out, tokens, gain, cots):
    rows, features = tokens.shape
    parts, count = rows // PART, len(cots)
    vmem, anywhere = pl.BlockSpec(memory_space=pltpu.VMEM), pl.BlockSpec(memory_space=pl.ANY)
    dma = pltpu.SemaphoreType.DMA
    everyone = jax.ShapeDtypeStruct((ndp, rows, features), bf16)
    low = pltpu.VMEM((rows, features), bf16)
    return pl.pallas_call(
        functools.partial(enter_kernel, ndp),
        out_shape=(jax.ShapeDtypeStruct((rows, features), f32), everyone, everyone),
        in_specs=[vmem] * (4 + count),
        out_specs=(vmem, anywhere, anywhere),
        scratch_shapes=[
            low, low, low, dma((parts,)), dma((parts,)), dma((parts,)), dma((ndp, parts)), dma((ndp, parts)),
            dma((count,)), dma((count,)), dma((count,)),
        ],
        compiler_params=pltpu.CompilerParams(
            collective_id=6, has_side_effects=True, vmem_limit_bytes=VMEM_LIMIT
        ),
        cost_estimate=cost(65),
        name="enter_mlp",
    )(mixed, all_out, tokens, gain, *cots)


def leave_kernel(
    ndp, cots_ref, to_gate_ref, to_up_ref, mixed_ref, gate_up_ref, down_ref, middle_ref, gain_ref,
    grads_ref, out_ref, grad_ref, low_ref, gain_out_ref,
    cot_s, to_gate_s, to_up_s, mixed_s, grads_s, out_s, grad_s, load_sem, grads_sem, out_sem, grad_sem,
    keep, core_out, core_in, side_out, side_in, mine, theirs, out_keep, out_core, out_core_in,
    core_sems, side_sems, mp_sems, out_sems,
):
    rows, features = middle_ref.shape
    piece = down_ref.shape[1]
    parts = rows // PART
    bits, masks = doubling(ndp)
    dp, z, mp = (lax.axis_index(a) for a in ("dp", "seq", "mp"))
    peers_barrier(ndp)

    def at(c):
        return pl.ds(pl.multiple_of(c * PART, PART), PART)

    def loads(c):
        slot = lax.rem(c, 2)
        pairs = ((cots_ref, cot_s), (to_gate_ref, to_gate_s), (to_up_ref, to_up_s), (mixed_ref, mixed_s))
        return [
            pltpu.make_async_copy(ref.at[:, at(c)], buffer.at[slot], load_sem.at[k, slot])
            for k, (ref, buffer) in enumerate(pairs)
        ]

    def store_grads(c):
        slot = lax.rem(c, 2)
        return pltpu.make_async_copy(grads_s.at[slot], grads_ref.at[:, at(c)], grads_sem.at[slot])

    def store_out(c):
        slot = lax.rem(c, 2)
        return pltpu.make_async_copy(out_s.at[slot], out_ref.at[:, at(c)], out_sem.at[slot])

    def store_grad(c):
        slot = lax.rem(c, 2)
        return pltpu.make_async_copy(grad_s.at[slot], grad_ref.at[at(c)], grad_sem.at[slot])

    def remote(src, dst, sems, index, target):
        return pltpu.make_async_remote_copy(
            src_ref=src, dst_ref=dst, send_sem=sems.at[(0, *index)], recv_sem=sems.at[(1, *index)],
            device_id=target, device_id_type=MESH,
        )

    def to_core(c):
        return remote(core_out.at[lax.rem(c, 2)], core_in.at[c], core_sems, (c,), (flip(dp, 1), z, mp))

    def out_to_core(c):
        return remote(out_core.at[lax.rem(c, 2)], out_core_in.at[c], out_sems, (c,), (flip(dp, 1), z, mp))

    def to_side(c, mask):
        bit = 1 << (mask.bit_length() - 1)
        k = mask // 2 - 1
        return remote(side_out.at[c, k], side_in.at[c, k], side_sems, (c, k), (flip(dp, bit), z, mp))

    def to_mp(c):
        return remote(mine.at[c], theirs.at[c], mp_sems, (c,), (dp, z, 1 - mp))

    for copy in loads(0):
        copy.start()
    gain_out_ref[...] = jnp.zeros_like(gain_out_ref)

    def compute(c):
        slot = lax.rem(c, 2)
        for copy in loads(c):
            copy.wait()

        @pl.when(c + 1 < parts)
        def _():
            for copy in loads(c + 1):
                copy.start()

        @pl.when(c >= 2)
        def _():
            store_grads(c - 2).wait()
            to_core(c - 2).wait_send()
            out_to_core(c - 2).wait_send()

        low_ref[at(c), :] = cot_s[slot, 0]
        grad_mixed = matmul(cot_s[slot].reshape(ndp * PART, features), down_ref[...]).reshape(ndp, PART, piece)
        grads_s[slot, :, :, :piece] = (grad_mixed * to_gate_s[slot].astype(f32)).astype(bf16)
        grads_s[slot, :, :, piece:] = (grad_mixed * to_up_s[slot].astype(f32)).astype(bf16)
        store_grads(c).start()
        total = contract(grads_s[slot].reshape(ndp * PART, 2 * piece), gate_up_ref[...])
        total = total.reshape(ndp, PART, features)
        for mask in range(0, ndp, 2):
            keep[lax.rem(c, 4), mask // 2] = total[mask]
            core_out[slot, mask // 2] = total[mask | 1].astype(bf16)
        to_core(c).start()
        total = contract(mixed_s[slot].reshape(ndp * PART, piece), down_ref[...])
        total = total.reshape(ndp, PART, features)
        for mask in range(0, ndp, 2):
            out_keep[slot, mask // 2] = total[mask]
            out_core[slot, mask // 2] = total[mask | 1].astype(bf16)
        out_to_core(c).start()

    def after_core(c):
        to_core(c).wait_recv()
        slot = lax.rem(c, 4)
        keep[slot, 0] += core_in[c, 0].astype(f32)
        for mask in range(ndp - 2, 0, -2):
            total = keep[slot, mask // 2] + core_in[c, mask // 2].astype(f32)
            bit = 1 << (mask.bit_length() - 1)
            for more in bits:
                if more > bit:
                    to_side(c, mask | more).wait_recv()
                    total = total + side_in[c, (mask | more) // 2 - 1].astype(f32)
            side_out[c, mask // 2 - 1] = total.astype(bf16)
            to_side(c, mask).start()

        @pl.when(c >= 2)
        def _():
            store_out(c - 2).wait()

        slot = lax.rem(c, 2)
        out_to_core(c).wait_recv()
        for k in range(ndp // 2):
            out_s[slot, k] = (out_keep[slot, k] + out_core_in[c, k].astype(f32)).astype(bf16)
        store_out(c).start()

    def after_side(c):
        total = keep[lax.rem(c, 4), 0]
        for bit in bits:
            to_side(c, bit).wait_recv()
            total = total + side_in[c, bit // 2 - 1].astype(f32)
        mine[c] = total.astype(bf16)
        to_mp(c).start()

    def after_mp(c):
        to_mp(c).wait_recv()

        @pl.when(c >= 2)
        def _():
            store_grad(c - 2).wait()

        grad = mine[c].astype(f32) + theirs[c].astype(f32)
        middle = middle_ref[at(c), :]
        scale = lax.rsqrt(jnp.mean(middle * middle, axis=-1, keepdims=True) + epsilon)
        normed = middle * scale
        grad_normed = grad * gain_ref[...]
        grad_middle = low_ref[at(c), :].astype(f32) + scale * (
            grad_normed - normed * jnp.mean(grad_normed * normed, axis=-1, keepdims=True)
        )
        grad_s[lax.rem(c, 2)] = grad_middle
        store_grad(c).start()
        low_ref[at(c), :] = grad_middle.astype(bf16)
        gain_out_ref[...] += jnp.sum((grad * normed).reshape(PART // 8, 8, features), axis=0)

    def turn(t, _):
        for lag, stage in ((0, compute), (1, after_core), (2, after_side), (4, after_mp)):
            pl.when((t >= lag) & (t < parts + lag))(functools.partial(stage, t - lag))
        return 0

    lax.fori_loop(0, parts + 4, turn, 0)
    for c in (parts - 2, parts - 1):
        store_grads(c).wait()
        store_out(c).wait()
        store_grad(c).wait()
        to_core(c).wait_send()
        out_to_core(c).wait_send()

    def finish(c, _):
        to_mp(c).wait_send()
        for mask in range(2, ndp, 2):
            to_side(c, mask).wait_send()
        return 0

    lax.fori_loop(0, parts, finish, 0)


def leave_mlp(ndp, cots, to_gate, to_up, mixed, gate_up, down, middle, gain):
    rows, features = middle.shape
    piece = down.shape[1]
    parts, evens = rows // PART, ndp // 2
    vmem, anywhere = pl.BlockSpec(memory_space=pltpu.VMEM), pl.BlockSpec(memory_space=pl.ANY)
    dma = pltpu.SemaphoreType.DMA
    low = functools.partial(pltpu.VMEM, dtype=bf16)
    thin = (parts, PART, features)
    return pl.pallas_call(
        functools.partial(leave_kernel, ndp),
        out_shape=(
            jax.ShapeDtypeStruct((ndp, rows, 2 * piece), bf16),
            jax.ShapeDtypeStruct((evens, rows, features), bf16),
            jax.ShapeDtypeStruct((rows, features), f32),
            jax.ShapeDtypeStruct((rows, features), bf16),
            jax.ShapeDtypeStruct((8, features), f32),
        ),
        in_specs=[anywhere] * 4 + [vmem] * 4,
        out_specs=(anywhere, anywhere, anywhere, vmem, vmem),
        scratch_shapes=[
            low((2, ndp, PART, features)),
            pltpu.VMEM((2, ndp, PART, piece), to_gate.dtype),
            pltpu.VMEM((2, ndp, PART, piece), to_up.dtype),
            low((2, ndp, PART, piece)),
            low((2, ndp, PART, 2 * piece)),
            low((2, evens, PART, features)),
            pltpu.VMEM((2, PART, features), f32),
            dma((4, 2)), dma((2,)), dma((2,)), dma((2,)),
            pltpu.VMEM((4, evens, PART, features), f32),
            low((2, evens, PART, features)), low((parts, evens, PART, features)),
            low((parts, evens - 1, PART, features)), low((parts, evens - 1, PART, features)),
            low(thin), low(thin),
            pltpu.VMEM((2, evens, PART, features), f32),
            low((2, evens, PART, features)), low((parts, evens, PART, features)),
            dma((2, parts)), dma((2, parts, evens - 1)), dma((2, parts)), dma((2, parts)),
        ],
        compiler_params=pltpu.CompilerParams(
            collective_id=7, has_side_effects=True, vmem_limit_bytes=VMEM_LIMIT
        ),
        cost_estimate=cost(75),
        name="leave_mlp",
    )(cots, to_gate, to_up, mixed, gate_up, down, middle, gain)


def everyone(ndp, values):
    masks = doubling(ndp)[1]
    by_mask = {}
    for mask, value in zip(masks, values):
        by_mask[mask], by_mask[mask | 1] = value, xor_permute(value, "dp", 1)
    return jnp.stack([by_mask[mask] for mask in range(ndp)])


def side_sum(ndp, value):
    return (value[0::2].astype(f32) + xor_permute(value[1::2], "dp", 1).astype(f32)).astype(bf16)


def halving(ndp, value, after=None):
    for bit in doubling(ndp)[0]:
        half = value.shape[0] // 2
        other = xor_permute(value[half:], "dp", bit)
        if after is not None:
            other, _ = lax.optimization_barrier((other, after))
        value = (value[:half].astype(f32) + other.astype(f32)).astype(bf16)
    return value[0]


def enter_mlp_plain(ndp, mixed, all_out, tokens, gain, cots):
    part = contract(mixed, all_out).astype(bf16)
    middle = tokens.astype(f32) + (part.astype(f32) + xor_permute(part, "mp", 1).astype(f32))
    normed = [(middle * norm_scale(middle) * gain).astype(bf16)]
    for bit in doubling(ndp)[0]:
        normed += [xor_permute(value, "dp", bit) for value in normed]
    return middle, everyone(ndp, normed), everyone(ndp, cots)


def leave_mlp_plain(ndp, cots, to_gate, to_up, mixed, gate_up, down, middle, gain):
    rows, features = middle.shape
    piece = down.shape[1]
    grad_mixed = matmul(cots.reshape(-1, features), down).reshape(ndp, rows, piece)
    grads = jnp.concatenate([grad_mixed * to_gate, grad_mixed * to_up], axis=-1).astype(bf16)
    total = contract(grads.reshape(-1, 2 * piece), gate_up).astype(bf16).reshape(ndp, rows, features)
    total = halving(ndp, side_sum(ndp, total))
    grad = total.astype(f32) + xor_permute(total, "mp", 1).astype(f32)
    scale = norm_scale(middle)
    normed, grad_normed = middle * scale, grad * gain
    grad_middle = cots[0].astype(f32) + scale * (
        grad_normed - normed * jnp.mean(grad_normed * normed, axis=-1, keepdims=True)
    )
    out = contract(mixed.reshape(-1, piece), down).astype(bf16).reshape(ndp, rows, features)
    gain_out = jnp.sum((grad * normed).reshape(rows // 8, 8, features), axis=0)
    return grads, side_sum(ndp, out), grad_middle, grad_middle.astype(bf16), gain_out


def on_device(
    ndp, nseq,
    tokens, doc_lengths, norm_gain, w_y, w_x, gate_a, gate_i, bias_a, bias_i, conv_w, conv_b,
    decay_param, w_out, mlp_gain, w_gate, w_up, w_down, cotangent,
):
    local_len, features = tokens.shape
    rows_here = w_y.shape[0]
    hidden_here = w_gate.shape[1]
    block = gate_a.shape[1]
    piece = hidden_here // ndp
    bits = [1 << k for k in range(ndp.bit_length() - 1)]

    def spread(value):
        values = [value]
        for bit in doubling(ndp)[0]:
            values += [xor_permute(v, "dp", bit) for v in values]
        return values

    def flat(value):
        return value.reshape(-1, value.shape[-1])

    def gather_mlp(value):
        value = value.reshape(ndp, rows_here, -1)
        return lax.all_gather(value, "seq", axis=1, tiled=True).reshape(features, -1)

    all_y, all_x, all_out, gate_rows, up_rows, down_rows = gather_weights(
        ndp, nseq, [w_y, w_x, w_out], [False, True, False], [w_gate, w_up, w_down], 3
    )
    gate_up = gather_mlp(jnp.concatenate([gate_rows, up_rows], axis=1))
    all_down = gather_mlp(down_rows)

    position = lax.axis_index("seq") * local_len + jnp.arange(local_len + PAD, dtype=jnp.int32)
    lengths_row = doc_lengths[0]
    starts = jnp.cumsum(lengths_row) - lengths_row
    resets = jnp.any(position[:, None] == starts[None, :], axis=1)
    doc_start = jnp.max(jnp.where(starts[None, :] <= position[:, None], starts[None, :], 0), axis=1)
    marks = jnp.stack(
        [1.0 - resets.astype(f32)] + [(position - lag >= doc_start).astype(f32) for lag in (1, 2, 3)]
    )
    marks = jnp.broadcast_to(marks[:, :, None], (4, local_len + PAD, LANES))
    vectors = jnp.concatenate(
        [conv_w, conv_b[None], bias_a[None], bias_i[None], jax.nn.softplus(-decay_param)[None]], axis=0
    )

    resid = tokens.astype(f32)
    scale_one = norm_scale(resid)
    acts_one = (resid * scale_one * norm_gain).astype(bf16)
    cots_ready, _ = lax.optimization_barrier((cotangent, all_y))
    mixed_rec, states, pxe, pre_y, rate, ig, conv_out = rec_forward(
        nseq, acts_one, all_x, all_y, marks, gate_a, gate_i, vectors
    )
    all_cots = spread(cots_ready)

    small_group = ndp <= 4
    middle, acts, cots = (enter_mlp if small_group else enter_mlp_plain)(
        ndp, mixed_rec, all_out, tokens, mlp_gain[None], all_cots
    )
    acts_flat, cots_flat = flat(acts), flat(cots)
    pre = matmul(acts_flat, gate_up)
    pre_gate, pre_up = pre[:, :piece], pre[:, piece:]
    gelu, slope = gelu_parts(pre_gate)
    mixed = (gelu * pre_up).astype(bf16)
    to_gate, to_up = (pre_up * slope).reshape(ndp, local_len, piece), gelu.reshape(ndp, local_len, piece)

    def rows_total(left, right):
        return contract_rows(left, right).astype(bf16).reshape(ndp, nseq * rows_here, -1)

    def reduce_mlp(total):
        return lax.psum_scatter(total, "seq", scatter_dimension=1, tiled=True)

    sum_down = reduce_mlp(rows_total(cots_flat, mixed))
    grads, out_sides, grad_middle, grad_middle_low, gain_two = (leave_mlp if small_group else leave_mlp_plain)(
        ndp, cots, to_gate, to_up, mixed.reshape(ndp, local_len, piece), gate_up, all_down, middle, mlp_gain[None]
    )
    total_gate_up, grad_middle_low = lax.optimization_barrier((rows_total(acts_flat, flat(grads)), grad_middle_low))
    sum_gate_up = reduce_mlp(total_gate_up)

    grad_pre_y, grad_pre_x, grad_gate_a, grad_gate_i, sums = rec_backward(
        nseq, grad_middle_low, all_out, marks, gate_a, gate_i, vectors, (pre_y, states, rate, pxe, ig, conv_out)
    )
    part = (contract(grad_pre_y, all_y) + contract(grad_pre_x, all_x)).astype(bf16)
    other = xor_permute(part, "mp", 1)
    out_part = halving(ndp, out_sides, grad_pre_y)
    other_out = xor_permute(out_part, "mp", 1)
    normed = resid * scale_one
    small = [
        grad_gate_a, grad_gate_i, sums, jnp.sum(part.astype(f32) * normed, axis=0), jnp.sum(gain_two, axis=0),
    ]
    sizes = [value.size // block for value in small]
    total_rows = -(-sum(sizes) // (16 * ndp * nseq)) * 16 * ndp * nseq
    small_rows = jnp.concatenate(
        [value.reshape(-1, block) for value in small] + [jnp.zeros((total_rows - sum(sizes), block), f32)], axis=0
    )
    small_sum, grad_w_y, grad_w_x, grad_w_out = reduce_weights(
        ndp, nseq, [acts_one, grad_middle_low],
        [(None, small_rows), (0, grad_pre_y), (0, grad_pre_x), (1, mixed_rec)], 4,
    )
    small_sum, sum_gate_up, other, other_out = lax.optimization_barrier((small_sum, sum_gate_up, other, other_out))
    (small_all,) = gather_weights(ndp, nseq, [small_sum.astype(bf16)], [False], [], 5)
    totals, begin = [], 0
    for value, size in zip(small, sizes):
        totals.append(small_all[begin : begin + size].astype(f32).reshape(value.shape))
        begin += size
    grad_gate_a, grad_gate_i, sums, gain_one, gain_two = totals
    gain_one = gain_one + xor_permute(gain_one, "mp", 1)

    grad_acts = part.astype(f32) + other.astype(f32)
    grad_normed = grad_acts * norm_gain
    input_grad = grad_middle + scale_one * (
        grad_normed - normed * jnp.mean(grad_normed * normed, axis=-1, keepdims=True)
    )

    output = (middle + (out_part.astype(f32) + other_out.astype(f32))).astype(bf16)

    def regroup(value):
        return lax.all_to_all(value, "dp", 0, 2, tiled=True)[0].astype(f32)

    grad_w_down = regroup(sum_down)
    grad_w_gate, grad_w_up = regroup(sum_gate_up[:, :, :piece]), regroup(sum_gate_up[:, :, piece:])
    return (
        output,
        input_grad,
        gain_one,
        grad_w_y,
        grad_w_x,
        grad_gate_a,
        grad_gate_i,
        sums[0],
        sums[1],
        sums[4:8],
        sums[3],
        sums[2] * jax.nn.sigmoid(-decay_param),
        grad_w_out,
        gain_two,
        grad_w_gate,
        grad_w_up,
        grad_w_down,
    )


def solution(mesh):
    rows, cols = P(("dp", "seq"), None), P(("dp", "seq"), "mp")
    return jax.shard_map(
        functools.partial(on_device, mesh.shape["dp"], mesh.shape["seq"]),
        mesh=mesh,
        in_specs=(
            rows, P("dp", None), P(), cols, cols, P("mp", None, None), P("mp", None, None), P("mp"), P("mp"),
            P(None, "mp"), P("mp"), P("mp"), cols, P(), cols, cols, cols, rows,
        ),
        out_specs=(
            rows, rows, P(), cols, cols, P("mp", None, None), P("mp", None, None), P("mp"), P("mp"),
            P(None, "mp"), P("mp"), P("mp"), cols, P(), cols, cols, cols,
        ),
        check_vma=False,
    )
```

```python
import functools

import jax
import jax.numpy as jnp
from jax import lax
from jax.experimental import pallas as pl
from jax.experimental.pallas import tpu as pltpu
from jax.sharding import PartitionSpec as P

epsilon = 1e-06
decay_scale = 8.0
MESH = pl.DeviceIdType.MESH
VMEM_LIMIT = 60 * 2**20
SEGMENTS = 8
PAD = 8
bf16 = jnp.bfloat16
f32 = jnp.float32


def xor_permute(value, axis, bit):
    count = lax.axis_size(axis)
    return lax.ppermute(value, axis, [(source, source ^ bit) for source in range(count)])


def matmul(left, right):
    return jnp.dot(left, right, preferred_element_type=f32)


def contract(left, right):
    return lax.dot_general(left, right, (((1,), (1,)), ((), ())), preferred_element_type=f32)


def contract_rows(left, right):
    return lax.dot_general(left, right, (((0,), (0,)), ((), ())), preferred_element_type=f32)


def norm_scale(values):
    return lax.rsqrt(jnp.mean(values * values, axis=-1, keepdims=True) + epsilon)


def gelu_parts(y):
    c = 0.7978845608028654
    u = c * (y + 0.044715 * y * y * y)
    t = jnp.tanh(u)
    half = 0.5 * (1.0 + t)
    slope = half + 0.5 * y * (1.0 - t * t) * (c * (1.0 + 3.0 * 0.044715 * y * y))
    return y * half, slope


def one_minus_square(log_decay, decay):
    y = -2.0 * log_decay
    series = 1.0 - y * (1.0 / 5.0)
    for k in (4, 3, 2):
        series = 1.0 - y * (1.0 / k) * series
    return jnp.where(y < 0.1, y * series, 1.0 - decay * decay)


def seq_barrier(nseq, ndp=1):
    dp, z, mp = (lax.axis_index(a) for a in ("dp", "seq", "mp"))
    barrier = pltpu.get_barrier_semaphore()
    for step in range(1, nseq):
        pl.semaphore_signal(
            barrier, inc=1, device_id=(dp, lax.rem(z + step, nseq), mp), device_id_type=MESH
        )
    for mask in range(1, ndp):
        pl.semaphore_signal(barrier, inc=1, device_id=(flip(dp, mask), z, mp), device_id_type=MESH)
    pl.semaphore_wait(barrier, nseq + ndp - 2)


def to_seq(src, dst, send_sem, recv_sem, target):
    dp, mp = (lax.axis_index(a) for a in ("dp", "mp"))
    return pltpu.make_async_remote_copy(
        src_ref=src,
        dst_ref=dst,
        send_sem=send_sem,
        recv_sem=recv_sem,
        device_id=(dp, target, mp),
        device_id_type=MESH,
    )


LANES = 128


def spread_lanes(value, width):
    return jnp.concatenate([value] * (width // value.shape[1]), axis=1)


def rec_forward_kernel(
    nseq, heads, block,
    acts_ref, wx_ref, wy_ref, marks_ref, ga_ref, gi_ref, vec_ref,
    mixed_ref, states_out, pxe_out, py_out, rate_out, ig_out, co_out,
    wy_s, states_s, pxe_s, py_s, rate_s, ig_s, co_s,
    a_s, b_s, tail_s, msg, got, state_in, halo, load_sem, store_sems, halo_send, halo_recv, end_send, end_recv,
):
    rows, width = mixed_ref.shape
    seg = rows // SEGMENTS
    z = lax.axis_index("seq")
    load = pltpu.make_async_copy(wy_ref, wy_s, load_sem)
    load.start()
    seq_barrier(nseq)

    def store(k, source, target):
        return pltpu.make_async_copy(source, target, store_sems.at[k])

    pairs = (
        (py_s, py_out), (pxe_s, pxe_out), (rate_s, rate_out), (ig_s, ig_out), (co_s, co_out), (states_s, states_out),
    )

    def block_cols(h):
        return pl.ds(pl.multiple_of(h * block, block), block)

    def project_x(h, _):
        product = matmul(acts_ref[...], wx_ref[:, block_cols(h)])
        pxe_s[pl.ds(PAD, rows), block_cols(h)] = product.astype(bf16).astype(f32)
        return 0

    lax.fori_loop(0, heads, project_x, 0)
    tail_s[...] = pxe_s[pl.ds(rows, PAD), :]

    def halo_copy(target):
        return to_seq(tail_s, halo, halo_send, halo_recv, target)

    @pl.when(z < nseq - 1)
    def _():
        halo_copy(z + 1).start()

    load.wait()

    def project_y(h, _):
        py_s[:, block_cols(h)] = matmul(acts_ref[...], wy_s[:, block_cols(h)])
        return 0

    lax.fori_loop(0, heads, project_y, 0)
    store(0, *pairs[0]).start()

    @pl.when(z == 0)
    def _():
        halo[...] = jnp.zeros_like(halo)

    @pl.when(z > 0)
    def _():
        halo_copy(z).wait_recv()

    pxe_s[pl.ds(0, PAD), :] = halo[...]
    store(1, *pairs[1]).start()

    def head(h, _):
        cols = block_cols(h)

        def part(r, _):
            at = pl.ds(pl.multiple_of(r * seg, seg), seg)
            window = pxe_s[pl.ds(pl.multiple_of(r * seg, seg), seg + PAD), cols]
            conv_out = vec_ref[4:5, cols] + vec_ref[0:1, cols] * window[PAD:]
            for lag in (1, 2, 3):
                shifted = pltpu.roll(window, lag, 0)[PAD:]
                conv_out = conv_out + vec_ref[lag : lag + 1, cols] * shifted * spread_lanes(marks_ref[lag, at, :], block)
            low = conv_out.astype(bf16)
            gate_r = matmul(low, ga_ref[h])
            gate_x = matmul(low, gi_ref[h])
            rate = jax.nn.sigmoid(gate_r + vec_ref[5:6, cols])
            ig = jax.nn.sigmoid(gate_x + vec_ref[6:7, cols])
            log_decay = -decay_scale * rate * vec_ref[7:8, cols]
            decay = jnp.exp(log_decay)
            mult = jnp.sqrt(one_minus_square(log_decay, decay))
            a_s[at, cols] = decay * spread_lanes(marks_ref[0, at, :], block)
            b_s[at, cols] = conv_out * ig * mult
            rate_s[at, cols] = rate
            ig_s[at, cols] = ig
            co_s[at, cols] = conv_out
            return 0

        lax.fori_loop(0, SEGMENTS, part, 0)
        return 0

    lax.fori_loop(0, heads, head, 0)
    for k in (2, 3, 4):
        store(k, *pairs[k]).start()
    row = lax.broadcasted_iota(jnp.int32, (8, width), 0)

    def turn(t, kept):
        prefix, state = kept
        at = pl.ds(pl.multiple_of(t * 8, 8), 8)
        decay, drive = a_s[at, :], b_s[at, :]
        for k in (1, 2, 4):
            inside = row >= k
            drive = decay * jnp.where(inside, pltpu.roll(drive, k, 0), 0.0) + drive
            decay = decay * jnp.where(inside, pltpu.roll(decay, k, 0), 1.0)
        drive = decay * state + drive
        decay = decay * prefix
        a_s[at, :] = decay
        b_s[at, :] = drive
        return decay[7:8], drive[7:8]

    one, zero = jnp.ones((1, width), f32), jnp.zeros((1, width), f32)
    prefix, state = lax.fori_loop(0, rows // 8, turn, (one, zero))
    msg[0:1, :] = prefix
    msg[1:2, :] = state
    msg[2:PAD, :] = jnp.zeros((PAD - 2, width), f32)
    for step in range(1, nseq):

        @pl.when(z + step < nseq)
        def _():
            to_seq(msg, got.at[z], end_send.at[step - 1], end_recv.at[z], z + step).start()

    state_in[...] = jnp.zeros_like(state_in)
    for source in range(nseq - 1):

        @pl.when(source < z)
        def _():
            to_seq(msg, got.at[source], end_send.at[0], end_recv.at[source], z).wait_recv()
            state_in[...] = got[source, 0:1, :] * state_in[...] + got[source, 1:2, :]

    states_s[pl.ds(0, PAD), :] = jnp.broadcast_to(state_in[...], (PAD, width))

    def finish(i, _):
        s, h = i // heads, lax.rem(i, heads)
        cols = block_cols(h)
        at = pl.ds(pl.multiple_of(s * seg, seg), seg)
        states = b_s[at, cols] + a_s[at, cols] * state_in[:, cols]
        states_s[pl.ds(pl.multiple_of(PAD + s * seg, PAD), seg), cols] = states
        mixed_ref[at, cols] = (states * gelu_parts(py_s[at, cols])[0]).astype(bf16)
        return 0

    lax.fori_loop(0, SEGMENTS * heads, finish, 0)
    store(5, *pairs[5]).start()

    @pl.when(z < nseq - 1)
    def _():
        halo_copy(z).wait_send()

    for step in range(1, nseq):

        @pl.when(z + step < nseq)
        def _():
            to_seq(msg, got.at[z], end_send.at[step - 1], end_recv.at[z], z).wait_send()

    for k, pair in enumerate(pairs):
        store(k, *pair).wait()


def rec_forward(nseq, acts, all_x, all_y, marks, gate_a, gate_i, vectors):
    rows, width = acts.shape[0], all_x.shape[1]
    heads, block = gate_a.shape[:2]
    vmem, anywhere = pl.BlockSpec(memory_space=pltpu.VMEM), pl.BlockSpec(memory_space=pl.ANY)
    big, ext = (rows, width), (rows + PAD, width)
    kept = (ext, ext, big, big, big, big)
    small = pltpu.VMEM((PAD, width), f32)
    dma = pltpu.SemaphoreType.DMA
    return pl.pallas_call(
        functools.partial(rec_forward_kernel, nseq, heads, block),
        out_shape=[jax.ShapeDtypeStruct(big, bf16)] + [jax.ShapeDtypeStruct(shape, f32) for shape in kept],
        in_specs=[vmem, vmem, anywhere] + [vmem] * 4,
        out_specs=[vmem] + [anywhere] * 6,
        scratch_shapes=[
            pltpu.VMEM(all_y.shape, bf16),
            *[pltpu.VMEM(shape, f32) for shape in kept],
            pltpu.VMEM(big, f32),
            pltpu.VMEM(big, f32),
            small,
            small,
            pltpu.VMEM((nseq, PAD, width), f32),
            pltpu.VMEM((1, width), f32),
            small,
            dma, dma((6,)), dma, dma, dma((nseq - 1,)), dma((nseq,)),
        ],
        compiler_params=pltpu.CompilerParams(
            collective_id=1, has_side_effects=True, vmem_limit_bytes=VMEM_LIMIT
        ),
        cost_estimate=cost(3),
        name="rec_forward",
    )(acts, all_x, all_y, marks, gate_a, gate_i, vectors)


def rec_backward_kernel(
    ndp, nseq, heads, block,
    low_ref, mixed_ref, out_ref, marks_ref, ga_ref, gi_ref, vec_ref, py_ref, states_ref, rate_ref, pxe_ref, ig_ref, co_ref,
    gpy_ref, gpx_ref, gga_ref, ggi_ref, sums_ref, ready_ref,
    py_s, states_s, rate_s, pxe_s, ig_s, co_s, w_s, b_s, g_s, gm_s, gc_s, gr_s, gx_s,
    msg, got, grad_in, head_s, load_sems, halo_send, halo_recv, end_send, end_recv,
    low_t, core_out, core_in, side_out, side_in, keep, core_sems, side_sems,
):
    rows, width = gpy_ref.shape
    seg = rows // SEGMENTS
    z = lax.axis_index("seq")
    loads = [
        pltpu.make_async_copy(source, target, load_sems.at[k])
        for k, (source, target) in enumerate(
            ((py_ref, py_s), (states_ref, states_s), (rate_ref, rate_s), (pxe_ref, pxe_s), (ig_ref, ig_s), (co_ref, co_s))
        )
    ]
    for load in loads:
        load.start()

    def transpose(k, _):
        at = pl.ds(pl.multiple_of(k * LANES, LANES), LANES)
        low_t[:, at] = low_ref[at, :].astype(f32).T.astype(bf16)
        return 0

    lax.fori_loop(0, rows // LANES, transpose, 0)
    seq_barrier(nseq, ndp)
    dp = lax.axis_index("dp")
    row_block = ready_ref.shape[1]

    def product(mask):
        return matmul(dp_rows(low_t, row_block * nseq, mask), mixed_ref[...])

    copies = Copies()
    weight = DpSum(
        ndp, nseq, product, keep, None, (core_out, core_in, side_out, side_in), (core_sems, side_sems), copies
    )
    weight.begin()
    for load in loads[:3]:
        load.wait()

    def block_cols(h):
        return pl.ds(pl.multiple_of(h * block, block), block)

    def first(h, _):
        cols = block_cols(h)
        gm_s[...] = matmul(low_ref[...], out_ref[:, cols])

        def part(s, _):
            at = pl.ds(pl.multiple_of(s * seg, seg), seg)
            gelu, slope = gelu_parts(py_s[at, cols])
            gm = gm_s[at, :]
            states = states_s[pl.ds(pl.multiple_of(PAD + s * seg, PAD), seg), cols]
            gpy_ref[at, cols] = (gm * states * slope).astype(bf16)
            decay = jnp.exp(-decay_scale * rate_s[at, cols] * vec_ref[7:8, cols])
            decay = decay * spread_lanes(marks_ref[0, at, :], block)
            grad = gm * gelu
            b_s[at, cols] = grad
            w_s[at, cols] = decay
            g_s[at, cols] = grad * decay
            return 0

        lax.fori_loop(0, SEGMENTS, part, 0)
        return 0

    lax.fori_loop(0, heads, first, 0)
    weight.to_side()
    row = lax.broadcasted_iota(jnp.int32, (8, width), 0)

    def turn(i, kept):
        suffix, owed = kept
        at = pl.ds(pl.multiple_of(rows - 8 - i * 8, 8), 8)
        decay, grad = w_s[at, :], g_s[at, :]
        for k in (1, 2, 4):
            inside = row < 8 - k
            grad = decay * jnp.where(inside, pltpu.roll(grad, 8 - k, 0), 0.0) + grad
            decay = decay * jnp.where(inside, pltpu.roll(decay, 8 - k, 0), 1.0)
        grad = decay * owed + grad
        decay = decay * suffix
        w_s[at, :] = decay
        g_s[at, :] = grad
        return decay[0:1], grad[0:1]

    one, zero = jnp.ones((1, width), f32), jnp.zeros((1, width), f32)
    suffix, owed = lax.fori_loop(0, rows // 8, turn, (one, zero))
    w_s[pl.ds(rows, PAD), :] = jnp.ones((PAD, width), f32)
    g_s[pl.ds(rows, PAD), :] = jnp.zeros((PAD, width), f32)
    msg[0:1, :] = suffix
    msg[1:2, :] = owed
    msg[2:PAD, :] = jnp.zeros((PAD - 2, width), f32)
    for step in range(1, nseq):

        @pl.when(z >= step)
        def _():
            to_seq(msg, got.at[z], end_send.at[step - 1], end_recv.at[z], z - step).start()

    for load in loads[3:]:
        load.wait()
    grad_in[...] = jnp.zeros_like(grad_in)
    for source in range(nseq - 1, 0, -1):

        @pl.when(source > z)
        def _():
            to_seq(msg, got.at[source], end_send.at[0], end_recv.at[source], z).wait_recv()
            grad_in[...] = got[source, 0:1, :] * grad_in[...] + got[source, 1:2, :]

    def fold(value):
        return jnp.sum(value.reshape(seg // 8, 8, block), axis=0)

    def head(h, _):
        cols = block_cols(h)
        shrink = vec_ref[7:8, cols]

        def part(s, sums):
            at = pl.ds(pl.multiple_of(s * seg, seg), seg)
            ahead = pl.ds(pl.multiple_of(s * seg, seg), seg + PAD)
            owed = g_s[ahead, cols] + w_s[ahead, cols] * grad_in[:, cols]
            carry = b_s[at, cols] + pltpu.roll(owed, seg + PAD - 1, 0)[:seg]
            before = pltpu.roll(states_s[ahead, cols], 1, 0)[PAD:]
            rate, ig, conv_out = rate_s[at, cols], ig_s[at, cols], co_s[at, cols]
            log_decay = -decay_scale * rate * shrink
            decay = jnp.exp(log_decay)
            square = one_minus_square(log_decay, decay)
            inverse = lax.rsqrt(square)
            gated = carry * ig
            direct = gated * (square * inverse)
            gated = gated * conv_out
            keep = spread_lanes(marks_ref[0, at, :], block)
            grad_log = carry * before * decay * keep - gated * (decay * decay) * inverse
            spread = grad_log * decay_scale * rate
            grad_r = -spread * shrink * (1.0 - rate)
            grad_x = direct * conv_out * (1.0 - ig)
            low_r, low_x = grad_r.astype(bf16), grad_x.astype(bf16)
            gr_s[at, :] = low_r
            gx_s[at, :] = low_x
            grad_conv = direct + contract(low_r, ga_ref[h]) + contract(low_x, gi_ref[h])
            gc_s[at, cols] = grad_conv
            window = pxe_s[ahead, cols]
            terms = [grad_r, grad_x, spread, grad_conv, grad_conv * window[PAD:]]
            for lag in (1, 2, 3):
                terms.append(grad_conv * spread_lanes(marks_ref[lag, at, :], block) * pltpu.roll(window, lag, 0)[PAD:])
            return tuple(total + fold(term) for total, term in zip(sums, terms))

        sums = lax.fori_loop(
            0, SEGMENTS, part, tuple(jnp.zeros((8, block), f32) for _ in range(8))
        )
        for k, total in enumerate(sums):
            sums_ref[k : k + 1, cols] = jnp.sum(total, axis=0, keepdims=True)
        low = co_s[:, cols].astype(bf16)
        gga_ref[h] = contract_rows(low, gr_s[...])
        ggi_ref[h] = contract_rows(low, gx_s[...])
        return 0

    lax.fori_loop(0, heads, head, 0)
    head_s[...] = gc_s[pl.ds(0, PAD), :]

    @pl.when(z > 0)
    def _():
        to_seq(head_s, gc_s.at[pl.ds(rows, PAD)], halo_send, halo_recv, z - 1).start()

    @pl.when(z < nseq - 1)
    def _():
        to_seq(head_s, gc_s.at[pl.ds(rows, PAD)], halo_send, halo_recv, z).wait_recv()

    @pl.when(z == nseq - 1)
    def _():
        gc_s[pl.ds(rows, PAD), :] = jnp.zeros((PAD, width), f32)

    def final(i, _):
        s, h = i // heads, lax.rem(i, heads)
        cols = block_cols(h)
        at = pl.ds(pl.multiple_of(s * seg, seg), seg)
        ahead = pl.ds(pl.multiple_of(s * seg, seg), seg + PAD)
        owed = gc_s[ahead, cols]
        grad = vec_ref[0:1, cols] * owed[:seg]
        for lag in (1, 2, 3):
            shifted = owed * spread_lanes(marks_ref[lag, ahead, :], block)
            shifted = pltpu.roll(shifted, seg + PAD - lag, 0)[:seg]
            grad = grad + vec_ref[lag : lag + 1, cols] * shifted
        gpx_ref[at, cols] = grad.astype(bf16)
        return 0

    lax.fori_loop(0, SEGMENTS * heads, final, 0)
    for step in far_first(nseq):

        def ready():
            ready_ref[z + step] = weight.with_core(step, 0).astype(bf16)

        under(in_line(nseq, step), ready)
    copies.finish()

    @pl.when(z > 0)
    def _():
        to_seq(head_s, gc_s.at[pl.ds(rows, PAD)], halo_send, halo_recv, z).wait_send()

    for step in range(1, nseq):

        @pl.when(z >= step)
        def _():
            to_seq(msg, got.at[z], end_send.at[step - 1], end_recv.at[z], z).wait_send()


def rec_backward(ndp, nseq, low, mixed, all_out, marks, gate_a, gate_i, vectors, kept):
    rows, width = low.shape[0], all_out.shape[1]
    row_block = all_out.shape[0] // (ndp * nseq)
    buffers, sems = dp_sum_shapes(ndp, nseq, row_block, width, True)
    heads, block = gate_a.shape[:2]
    vmem, anywhere = pl.BlockSpec(memory_space=pltpu.VMEM), pl.BlockSpec(memory_space=pl.ANY)
    grads = jax.ShapeDtypeStruct((rows, width), bf16)
    gates = jax.ShapeDtypeStruct(gate_a.shape, f32)
    small = pltpu.VMEM((PAD, width), f32)
    ext = pltpu.VMEM((rows + PAD, width), f32)
    dma = pltpu.SemaphoreType.DMA
    return pl.pallas_call(
        functools.partial(rec_backward_kernel, ndp, nseq, heads, block),
        out_shape=(
            grads, grads, gates, gates, jax.ShapeDtypeStruct((8, width), f32),
            jax.ShapeDtypeStruct((nseq, row_block, width), bf16),
        ),
        in_specs=[vmem] * 7 + [anywhere] * len(kept),
        out_specs=[vmem] * 6,
        scratch_shapes=[
            *[pltpu.VMEM(k.shape, k.dtype) for k in kept],
            ext,
            pltpu.VMEM((rows, width), f32),
            ext,
            pltpu.VMEM((rows, block), f32),
            ext,
            pltpu.VMEM((rows, block), bf16),
            pltpu.VMEM((rows, block), bf16),
            small,
            pltpu.VMEM((nseq, PAD, width), f32),
            pltpu.VMEM((1, width), f32),
            small,
            dma((len(kept),)), dma, dma, dma((nseq - 1,)), dma((nseq,)),
            pltpu.VMEM(low.shape[::-1], bf16), *buffers, *sems,
        ],
        compiler_params=pltpu.CompilerParams(
            collective_id=2, has_side_effects=True, vmem_limit_bytes=VMEM_LIMIT
        ),
        cost_estimate=cost(20),
        name="rec_backward",
    )(low, mixed, all_out, marks, gate_a, gate_i, vectors, *kept)


def flip(index, mask):
    bit = 1
    while bit <= mask:
        if mask & bit:
            index = index + bit - 2 * bit * lax.rem(index // bit, 2)
        bit *= 2
    return index


def neighbour_barrier(ndp, nseq):
    dp, z, mp = (lax.axis_index(a) for a in ("dp", "seq", "mp"))
    barrier = pltpu.get_barrier_semaphore()

    def greet(target):
        pl.semaphore_signal(barrier, inc=1, device_id=target, device_id_type=MESH)

    for mask in range(1, ndp):
        greet((flip(dp, mask), z, mp))

    @pl.when(z > 0)
    def _():
        greet((dp, z - 1, mp))

    @pl.when(z < nseq - 1)
    def _():
        greet((dp, z + 1, mp))

    neighbours = lax.div(z + nseq - 1, nseq) + lax.div(2 * nseq - 2 - z, nseq)
    pl.semaphore_wait(barrier, ndp - 1 + neighbours)


class Copies:
    def __init__(self):
        self.sent = []

    def start(self, here, make):
        under(here, lambda: make().start())
        self.sent.append((here, make))

    def finish(self):
        for here, make in self.sent:
            under(here, lambda: make().wait_send())


def under(here, body):
    if here is None:
        body()
    else:
        pl.when(here)(body)


def in_line(nseq, step):
    z = lax.axis_index("seq")
    if step == 0:
        return None
    return z + step < nseq if step > 0 else z + step >= 0


class Gather:
    def __init__(self, ndp, nseq, side_first, shards, wholes, send, recv):
        self.ndp, self.nseq, self.side_first = ndp, nseq, side_first
        self.shards, self.wholes, self.send, self.recv = shards, wholes, send, recv
        self.bits, self.masks = doubling(ndp)
        self.copies = Copies()
        self.dp, self.z, self.mp = (lax.axis_index(a) for a in ("dp", "seq", "mp"))

    def place(self, i, step, mask):
        rows = self.shards[i].shape[0]
        block = flip(self.dp, mask) * self.nseq + self.z + step
        return pl.ds(pl.multiple_of(block * rows, rows), rows)

    def copy(self, i, step, mask, there, mask_there, target):
        whole = self.wholes[i].at[self.place(i, step, mask)]
        index = (i, there + self.nseq - 1, mask_there)
        return pltpu.make_async_remote_copy(
            src_ref=self.shards[i] if step == 0 and mask == 0 and target is not None else whole,
            dst_ref=whole,
            send_sem=self.send.at[index],
            recv_sem=self.recv.at[index],
            device_id=(self.dp, self.z, self.mp) if target is None else target,
            device_id_type=MESH,
        )

    def along(self, i, step, mask):
        for way in (1, -1):
            if step * way > 0:
                continue
            near = in_line(self.nseq, way)
            here = near if step == 0 else near & in_line(self.nseq, step)
            target = (self.dp, self.z + way, self.mp)
            self.copies.start(here, functools.partial(self.copy, i, step, mask, step - way, mask, target))

    def across(self, i, step, mask, bit):
        target = (flip(self.dp, bit), self.z, self.mp)
        self.copies.start(
            in_line(self.nseq, step), functools.partial(self.copy, i, step, mask, step, mask | bit, target)
        )

    def go_on(self, i, step, mask):
        if mask & 1:
            return
        lower = [bit for bit in self.bits if mask == 0 or bit < mask & -mask]
        if self.side_first[i]:
            if step == 0:
                for bit in lower:
                    self.across(i, step, mask, bit)
            self.along(i, step, mask)
        else:
            if mask == 0:
                self.along(i, step, mask)
            for bit in lower:
                self.across(i, step, mask, bit)
        self.across(i, step, mask, 1)

    def arrive(self, i, step, mask):
        under(in_line(self.nseq, step), lambda: self.copy(i, step, mask, step, mask, None).wait_recv())
        self.go_on(i, step, mask)

    def both(self, i, distance, mask):
        for step in sorted({-distance, distance}):
            self.arrive(i, step, mask)

    def others(self, i):
        for mask in self.masks:
            for step in range(1 - self.nseq, self.nseq):
                self.arrive(i, step, mask | 1)


def gather_kernel(ndp, nseq, count, joined, tokens_ref, gain_ref, *refs):
    shards, wide, refs = refs[:count], refs[count : count + 3], refs[count + 3 :]
    wholes, refs = refs[:count], refs[count:]
    pieces, refs = (refs[:1] * 2, refs[1:]) if joined else (refs[:2], refs[2:])
    line, acts_ref, acts_t_ref, local_sem, send, recv, piece_send, piece_recv, line_send, line_recv = refs
    dp, z, mp = (lax.axis_index(a) for a in ("dp", "seq", "mp"))
    rows = shards[0].shape[0]
    piece_cols = line.shape[2]
    flow = Gather(ndp, nseq, [False] * count, shards, wholes, send, recv)

    def piece_place(k, block):
        if k == 2:
            return line.at[block, pl.ds(pl.multiple_of(z * rows, rows), rows)]
        at = pl.ds(pl.multiple_of(block * rows, rows), rows)
        return pieces[k].at[at, pl.ds(k * piece_cols, piece_cols)] if joined else pieces[k].at[at]

    def piece_copy(k, mask):
        cols = pl.ds(pl.multiple_of(flip(dp, mask) * piece_cols, LANES), piece_cols)
        src = wide[k].at[:, cols] if joined else wide[k].at[flip(dp, mask)]
        if mask == 0:
            return pltpu.make_async_copy(src, piece_place(k, dp), local_sem.at[count + k])
        return pltpu.make_async_remote_copy(
            src_ref=src, dst_ref=piece_place(k, dp), send_sem=piece_send.at[k, mask],
            recv_sem=piece_recv.at[k, mask], device_id=(flip(dp, mask), z, mp), device_id_type=MESH,
        )

    def send_pieces(k):
        for mask in range(ndp):
            piece_copy(k, mask).start()

    def pieces_here(k):
        piece_copy(k, 0).wait()
        for mask in range(1, ndp):
            place = piece_place(k, flip(dp, mask))
            pltpu.make_async_remote_copy(
                src_ref=place, dst_ref=place, send_sem=piece_send.at[k, mask],
                recv_sem=piece_recv.at[k, mask], device_id=(dp, z, mp), device_id_type=MESH,
            ).wait_recv()

    def line_copy(step, there, target):
        place = line.at[:, pl.ds(pl.multiple_of((z + step) * rows, rows), rows)]
        return pltpu.make_async_remote_copy(
            src_ref=place, dst_ref=place, send_sem=line_send.at[there + nseq - 1],
            recv_sem=line_recv.at[there + nseq - 1], device_id=target, device_id_type=MESH,
        )

    def line_on(step):
        for way in (1, -1):
            if step * way <= 0:
                near = in_line(nseq, way)
                here = near if step == 0 else near & in_line(nseq, step)
                flow.copies.start(here, functools.partial(line_copy, step, step - way, (dp, z + way, mp)))

    def line_both(distance):
        for step in (-distance, distance):
            under(in_line(nseq, step), lambda: line_copy(step, step, (dp, z, mp)).wait_recv())
            line_on(step)

    def own(i):
        return pltpu.make_async_copy(shards[i], wholes[i].at[flow.place(i, 0, 0)], local_sem.at[i])

    neighbour_barrier(ndp, nseq)
    send_pieces(2)
    for i in range(count):
        flow.go_on(i, 0, 0)
    for i in range(count):
        own(i).start()

    def norm(c, _):
        at = pl.ds(pl.multiple_of(c * LANES, LANES), LANES)
        values = tokens_ref[at, :].astype(f32)
        scale = lax.rsqrt(jnp.mean(values * values, axis=-1, keepdims=True) + epsilon)
        acts = values * scale * gain_ref[...]
        acts_ref[at, :] = acts.astype(bf16)
        acts_t_ref[:, at] = acts.T.astype(bf16)
        return 0

    lax.fori_loop(0, tokens_ref.shape[0] // LANES, norm, 0)
    pieces_here(2)
    line_on(0)
    sides = flow.masks[1:]
    for step in range(1, nseq):
        if step < 3:
            send_pieces(step - 1)
        for i in range(count):
            flow.both(i, step, 0)
        line_both(step)
        for i in range(count):
            for mask in sides:
                flow.both(i, step - 1, mask)
    for i in range(count):
        for mask in sides:
            flow.both(i, nseq - 1, mask)
    for i in range(count):
        flow.others(i)
    for k in (0, 1):
        pieces_here(k)
    for i in range(count):
        own(i).wait()
    for k in range(3):
        for mask in range(1, ndp):
            piece_copy(k, mask).wait_send()
    flow.copies.finish()


def gather_weights(ndp, nseq, tokens, gain, shards, wide):
    rows = shards[0].shape[0]
    count = len(shards)
    piece = wide[0].shape[1] // ndp
    joined = piece % LANES == 0
    if not joined:
        wide = [jnp.swapaxes(w.reshape(rows, ndp, piece), 0, 1) for w in wide]
    dma = pltpu.SemaphoreType.DMA
    vmem, anywhere = pl.BlockSpec(memory_space=pltpu.VMEM), pl.BlockSpec(memory_space=pl.ANY)
    pairs = [(ndp * rows, 2 * piece)] if joined else [(ndp * rows, piece)] * 2
    *wholes, line, acts, acts_t = pl.pallas_call(
        functools.partial(gather_kernel, ndp, nseq, count, joined),
        out_shape=[jax.ShapeDtypeStruct((ndp * nseq * rows, s.shape[1]), s.dtype) for s in shards]
        + [jax.ShapeDtypeStruct(shape, bf16) for shape in pairs]
        + [jax.ShapeDtypeStruct((ndp, nseq * rows, piece), bf16)]
        + [jax.ShapeDtypeStruct(tokens.shape, bf16), jax.ShapeDtypeStruct(tokens.shape[::-1], bf16)],
        in_specs=[vmem] * 2 + [anywhere] * (count + 3),
        out_specs=[anywhere] * (count + len(pairs) + 1) + [vmem] * 2,
        scratch_shapes=[
            dma((count + 3,)), dma((count, 2 * nseq - 1, ndp)), dma((count, 2 * nseq - 1, ndp)),
            dma((3, ndp)), dma((3, ndp)), dma((2 * nseq - 1,)), dma((2 * nseq - 1,)),
        ],
        compiler_params=pltpu.CompilerParams(
            collective_id=3, has_side_effects=True, vmem_limit_bytes=VMEM_LIMIT
        ),
        cost_estimate=cost(3),
        name="gather_weights",
    )(tokens, gain, *shards, *wide)
    wholes, pairs = wholes[:count], wholes[count:]
    return wholes, jnp.concatenate(pairs, axis=1), line.reshape(-1, piece), acts, acts_t


class DpSum:
    def __init__(self, ndp, nseq, product, keep, block, buffers, sems, copies):
        self.ndp, self.nseq, self.copies = ndp, nseq, copies
        self.product, self.keep, self.block = product, keep, block
        self.core_out, self.core_in, self.side_out, self.side_in = buffers
        self.core_sems, self.side_sems = sems
        self.rows = self.core_out.shape[2]
        self.evens = list(range(0, ndp, 2))
        self.bits = doubling(ndp)[0]
        self.dp, self.z, self.mp = (lax.axis_index(a) for a in ("dp", "seq", "mp"))

    def remote(self, out, into, sems, at, bit):
        return pltpu.make_async_remote_copy(
            src_ref=out.at[at], dst_ref=into.at[at], send_sem=sems.at[(0, *at)], recv_sem=sems.at[(1, *at)],
            device_id=(flip(self.dp, bit), self.z, self.mp), device_id_type=MESH,
        )

    def core(self, step, mask):
        return self.remote(self.core_out, self.core_in, self.core_sems, (self.z + step, mask // 2), 1)

    def side(self, step, mask, bit):
        return self.remote(self.side_out, self.side_in, self.side_sems, (self.z + step, mask // 2 - 1), bit)

    def begin(self):
        for mask in self.evens:
            total = self.product(mask | 1).astype(bf16)
            for z in range(self.nseq):
                self.core_out[z, mask // 2] = total[z * self.rows : (z + 1) * self.rows]
        for step in far_first(self.nseq):
            for mask in self.evens:
                self.copies.start(in_line(self.nseq, step), functools.partial(self.core, step, mask))
        if self.keep is not None:
            for mask in self.evens:
                total = self.product(mask)
                for z in range(self.nseq):
                    self.keep[z, mask // 2] = total[z * self.rows : (z + 1) * self.rows]

    def with_core(self, step, mask):
        self.core(step, mask).wait_recv()
        at = (self.z + step, mask // 2)
        total = self.keep[at] if self.keep is not None else self.block(step, mask)
        total = total + self.core_in[at].astype(f32)
        for more in self.bits:
            if mask == 0 or more > mask:
                self.side(step, mask | more, more).wait_recv()
                total = total + self.side_in[self.z + step, (mask | more) // 2 - 1].astype(f32)
        return total

    def to_side(self):
        for step in far_first(self.nseq):
            for mask in self.evens[:0:-1]:
                bit = 1 << (mask.bit_length() - 1)

                def work():
                    self.side_out[self.z + step, mask // 2 - 1] = self.with_core(step, mask).astype(bf16)

                under(in_line(self.nseq, step), work)
                self.copies.start(in_line(self.nseq, step), functools.partial(self.side, step, mask, bit))


def dp_rows(ref, rows, mask):
    return ref[pl.ds(pl.multiple_of(flip(lax.axis_index("dp"), mask) * rows, rows), rows), :]


def far_first(nseq):
    return [step for k in range(nseq - 1, 0, -1) for step in (k, -k)] + [0]


def dp_sum_shapes(ndp, nseq, rows, width, keep):
    dma, evens = pltpu.SemaphoreType.DMA, ndp // 2
    kept = [pltpu.VMEM((nseq, evens, rows, width), f32)] if keep else []
    return [
        pltpu.VMEM((nseq, lead, rows, width), bf16) for lead in (evens, evens, evens - 1, evens - 1)
    ] + kept, [dma((2, nseq, evens)), dma((2, nseq, evens - 1))]


def reduce_kernel(ndp, nseq, kinds, moves, *refs):
    lefts = max(kind[0] for kind in kinds if kind[0] is not None) + 1
    left_refs, refs = refs[:lefts], refs[lefts:]
    count = len(kinds)
    summed = [i for i in range(count) if kinds[i][0] != -1]
    rights, sources, refs = refs[:count], refs[count : count + moves], refs[count + moves :]
    all_ref, outs, moved = refs[0], refs[1:count], refs[count : count + moves]
    refs = refs[count + moves :]
    parts = {}
    copies = Copies()
    dp, z, mp = (lax.axis_index(a) for a in ("dp", "seq", "mp"))
    for i in summed:
        left, _, rows = kinds[i]
        buffers, refs = refs[:4], refs[4:]
        keep = None
        if left is not None:
            keep, refs = refs[0], refs[1:]
        sems, refs = refs[:2], refs[2:]

        def product(i, mask):
            left, _, rows = kinds[i]
            taken = dp_rows(rights[i] if left is None else left_refs[left], rows * nseq, mask)
            return taken if left is None else matmul(taken, rights[i][...])

        def block(i, step, mask):
            rows = kinds[i][2]
            start = pl.multiple_of((flip(dp, mask) * nseq + z + step) * rows, rows)
            return rights[i][pl.ds(start, rows), :]

        parts[i] = DpSum(
            ndp, nseq, functools.partial(product, i), keep, functools.partial(block, i), buffers, sems, copies
        )
    flow_out, up_in, down_in, refs = refs[:count], refs[count : 2 * count], refs[2 * count : 3 * count], refs[3 * count :]
    held, refs = refs[:moves], refs[moves:]
    acc, shard, flow_sems, up_sems, down_sems, send, recv, move_send, move_recv = refs
    moving = Regroup(ndp, sources, held, moved, move_send, move_recv)
    order = far_first(nseq)

    def flow(i, step, way):
        into, sems = (up_in, up_sems) if way > 0 else (down_in, down_sems)
        return pltpu.make_async_remote_copy(
            src_ref=flow_out[i].at[z + step], dst_ref=into[i].at[z + step],
            send_sem=flow_sems.at[i, z + step], recv_sem=sems.at[i, z + step],
            device_id=(dp, z + way, mp), device_id_type=MESH,
        )

    spread = Gather(ndp, nseq, [False], [shard], [all_ref], send, recv)
    sides = spread.masks[1:]

    def pass_on(i, step):
        spot = (pl.ds(0, kinds[i][2]), pl.ds(0, kinds[i][1]))

        def work():
            acc[spot] = parts[i].with_core(step, 0) if i in parts else rights[i][z + step].astype(f32)

            def add(into, way):
                flow(i, step, way).wait_recv()
                acc[spot] += into[i][z + step].astype(f32)

            if step >= 0:
                pl.when(z > 0)(lambda: add(up_in, 1))
            if step <= 0:
                pl.when(z < nseq - 1)(lambda: add(down_in, -1))
            if step:
                flow_out[i][z + step] = acc[spot].astype(bf16)
            elif i:
                outs[i - 1][...] = acc[spot]
            else:
                shard[...] = acc[spot].astype(bf16)
                all_ref[spread.place(0, 0, 0), :] = shard[...]

        under(in_line(nseq, step), work)
        if step:
            copies.start(in_line(nseq, step), functools.partial(flow, i, step, 1 if step > 0 else -1))

    def along(items, distance):
        for i in items:
            for step in (distance, -distance):
                pass_on(i, step)

    ready = [i for i in range(1, count) if i not in parts]
    products = [i for i in range(1, count) if i in parts]
    neighbour_barrier(ndp, nseq)
    along(ready, nseq - 1)
    parts[0].begin()
    for k, i in enumerate(products):
        parts[i].begin()
        if k == 0:
            parts[0].to_side()
        parts[i].to_side()
        if nseq - 2 - k > 0:
            along(ready, nseq - 2 - k)
    for distance in range(nseq - 2 - len(products), 0, -1):
        along(ready, distance)
    moving.start()
    for step in order:
        pass_on(0, step)
    spread.go_on(0, 0, 0)
    for k, i in enumerate(products):
        for distance in range(nseq - 1, 0, -1):
            along([i], distance)
        if k + 1 < nseq:
            spread.both(0, k + 1, 0)
    for i in ready + products:
        pass_on(i, 0)
    for distance in range(len(products) + 1, nseq):
        spread.both(0, distance, 0)
    for mask in sides:
        for distance in range(nseq):
            spread.both(0, distance, mask)
    moving.finish()
    spread.others(0)
    spread.copies.finish()
    copies.finish()


def reduce_weights(ndp, nseq, lefts, rights, values):
    blocks = ndp * nseq
    kinds = [
        (k, r.shape[-1], r.shape[1] if k == -1 else (r if k is None else lefts[k]).shape[0] // blocks)
        for k, r in rights
    ]
    count = len(rights)
    vmem = pl.BlockSpec(memory_space=pltpu.VMEM)
    dma = pltpu.SemaphoreType.DMA
    first_rows, first_width = kinds[0][2], kinds[0][1]
    scratch = []
    for left, width, rows in kinds:
        if left != -1:
            scratch += sum(dp_sum_shapes(ndp, nseq, rows, width, left is not None), [])
    for _ in range(3):
        scratch += [pltpu.VMEM((nseq, rows, width), bf16) for _, width, rows in kinds]
    moves = len(values)
    scratch += [pltpu.VMEM(value.shape, value.dtype) for value in values]
    return pl.pallas_call(
        functools.partial(reduce_kernel, ndp, nseq, kinds, moves),
        out_shape=[jax.ShapeDtypeStruct((first_rows * blocks, first_width), bf16)]
        + [jax.ShapeDtypeStruct((rows, width), f32) for _, width, rows in kinds[1:]]
        + [regrouped(value) for value in values],
        in_specs=[vmem] * (len(lefts) + count + moves),
        out_specs=[vmem] * (count + moves),
        scratch_shapes=[
            *scratch,
            pltpu.VMEM((max(kind[2] for kind in kinds), max(kind[1] for kind in kinds)), f32),
            pltpu.VMEM((first_rows, first_width), bf16),
            dma((count, nseq)), dma((count, nseq)), dma((count, nseq)),
            dma((1, 2 * nseq - 1, ndp)), dma((1, 2 * nseq - 1, ndp)),
            dma((max(moves, 1), ndp)), dma((max(moves, 1), ndp)),
        ],
        compiler_params=pltpu.CompilerParams(
            collective_id=4, has_side_effects=True, vmem_limit_bytes=VMEM_LIMIT
        ),
        cost_estimate=cost(3),
        name="reduce_weights",
    )(*lefts, *[r for _, r in rights], *values)


class Regroup:
    def __init__(self, ndp, sources, held, outs, send, recv):
        self.ndp, self.sources, self.held, self.outs, self.send, self.recv = ndp, sources, held, outs, send, recv
        self.dp, self.z, self.mp = (lax.axis_index(a) for a in ("dp", "seq", "mp"))
        self.all = [(k, mask) for k in range(len(sources)) for mask in range(1, ndp)]

    def copy(self, k, mask):
        return pltpu.make_async_remote_copy(
            src_ref=self.sources[k].at[flip(self.dp, mask)], dst_ref=self.held[k].at[mask],
            send_sem=self.send.at[k, mask], recv_sem=self.recv.at[k, mask],
            device_id=(flip(self.dp, mask), self.z, self.mp), device_id_type=MESH,
        )

    def place(self, k, mask, value):
        width = value.shape[1]
        cols = pl.ds(pl.multiple_of(flip(self.dp, mask) * width, LANES), width)
        self.outs[k][:, cols] = value.astype(f32)

    def start(self):
        for item in self.all:
            self.copy(*item).start()

    def finish(self):
        for k, source in enumerate(self.sources):
            self.place(k, 0, source[self.dp])
        for k, mask in self.all:
            self.copy(k, mask).wait_recv()
            self.place(k, mask, self.held[k][mask])
        for item in self.all:
            self.copy(*item).wait_send()


def regroup_kernel(ndp, count, *refs):
    barrier = pltpu.get_barrier_semaphore()
    dp, z, mp = (lax.axis_index(a) for a in ("dp", "seq", "mp"))
    for mask in range(1, ndp):
        pl.semaphore_signal(barrier, inc=1, device_id=(flip(dp, mask), z, mp), device_id_type=MESH)
    pl.semaphore_wait(barrier, ndp - 1)
    moving = Regroup(ndp, refs[:count], refs[2 * count : 3 * count], refs[count : 2 * count], *refs[3 * count :])
    moving.start()
    moving.finish()


def regroup_plain(value):
    return lax.all_to_all(value, "dp", 0, 2, tiled=True)[0].astype(f32)


def regrouped(value):
    ndp, rows, width = value.shape
    return jax.ShapeDtypeStruct((rows, ndp * width), f32)


def regroup(ndp, values):
    if any(value.shape[2] % LANES for value in values):
        return [regroup_plain(value) for value in values]
    count = len(values)
    vmem = pl.BlockSpec(memory_space=pltpu.VMEM)
    dma = pltpu.SemaphoreType.DMA
    return pl.pallas_call(
        functools.partial(regroup_kernel, ndp, count),
        out_shape=[regrouped(value) for value in values],
        in_specs=[vmem] * count,
        out_specs=[vmem] * count,
        scratch_shapes=[
            *[pltpu.VMEM(v.shape, v.dtype) for v in values], dma((count, ndp)), dma((count, ndp)),
        ],
        compiler_params=pltpu.CompilerParams(
            collective_id=8, has_side_effects=True, vmem_limit_bytes=VMEM_LIMIT
        ),
        cost_estimate=cost(3),
        name="regroup",
    )(*values)


PART = 64


def cost(us):
    return pl.CostEstimate(flops=int(us * 1e9), bytes_accessed=int(us * 1e5), transcendentals=0)


def peers_barrier(ndp):
    dp, z, mp = (lax.axis_index(a) for a in ("dp", "seq", "mp"))
    barrier = pltpu.get_barrier_semaphore()
    for mask in range(1, ndp):
        pl.semaphore_signal(barrier, inc=1, device_id=(flip(dp, mask), z, mp), device_id_type=MESH)
    pl.semaphore_signal(barrier, inc=1, device_id=(dp, z, 1 - mp), device_id_type=MESH)
    pl.semaphore_wait(barrier, ndp)


def doubling(ndp):
    bits = [1 << k for k in range(1, ndp.bit_length() - 1)][::-1]
    masks = [0]
    for bit in bits:
        masks += [mask | bit for mask in masks]
    return bits, masks


def enter_kernel(
    ndp, mixed_ref, out_ref, tokens_ref, gain_ref, *refs
):
    bits, masks = doubling(ndp)
    cots, refs = refs[: len(masks)], refs[len(masks) :]
    middle_ref, acts_ref, all_cots = refs[:3]
    mine, theirs, normed, mine_sem, theirs_sem, own_sem, send, recv, cot_own, cot_send, cot_recv = refs[3:]
    rows = mixed_ref.shape[0]
    parts = rows // PART
    dp, z, mp = (lax.axis_index(a) for a in ("dp", "seq", "mp"))
    peers_barrier(ndp)

    def at(c):
        return pl.ds(pl.multiple_of(c * PART, PART), PART)

    def exchange(c):
        return pltpu.make_async_remote_copy(
            src_ref=mine.at[at(c)], dst_ref=theirs.at[at(c)], send_sem=mine_sem.at[c], recv_sem=theirs_sem.at[c],
            device_id=(dp, z, 1 - mp), device_id_type=MESH,
        )

    def hand(c, mask, bit):
        return pltpu.make_async_remote_copy(
            src_ref=acts_ref.at[mask, at(c)] if mask else normed.at[at(c)],
            dst_ref=acts_ref.at[mask | bit, at(c)],
            send_sem=send.at[mask | bit, c],
            recv_sem=recv.at[mask | bit, c],
            device_id=(flip(dp, bit), z, mp),
            device_id_type=MESH,
        )

    def own(c):
        return pltpu.make_async_copy(normed.at[at(c)], acts_ref.at[0, at(c)], own_sem.at[c])

    def cot_copy(k):
        return pltpu.make_async_copy(cots[k], all_cots.at[masks[k]], cot_own.at[k])

    def cot_hand(k):
        return pltpu.make_async_remote_copy(
            src_ref=cots[k], dst_ref=all_cots.at[masks[k] | 1], send_sem=cot_send.at[k], recv_sem=cot_recv.at[k],
            device_id=(flip(dp, 1), z, mp), device_id_type=MESH,
        )

    def project(k, _):
        several = pl.ds(pl.multiple_of(k * 4 * PART, 4 * PART), 4 * PART)
        mine[several, :] = contract(mixed_ref[several, :], out_ref[...]).astype(bf16)
        for c in range(4):
            exchange(4 * k + c).start()
        return 0

    lax.fori_loop(0, parts // 4, project, 0)
    for k in range(len(masks)):
        cot_copy(k).start()
        cot_hand(k).start()

    def norm(c, _):
        exchange(c).wait_recv()
        both = mine[at(c), :].astype(f32) + theirs[at(c), :].astype(f32)
        middle = tokens_ref[at(c), :].astype(f32) + both
        middle_ref[at(c), :] = middle
        scale = lax.rsqrt(jnp.mean(middle * middle, axis=-1, keepdims=True) + epsilon)
        normed[at(c), :] = (middle * scale * gain_ref[...]).astype(bf16)
        own(c).start()
        for bit in bits + [1]:
            hand(c, 0, bit).start()
        return 0

    lax.fori_loop(0, parts, norm, 0)
    for mask in masks[1:]:

        def pass_on(c, _):
            hand(c, mask & (mask - 1), mask & -mask).wait_recv()
            for bit in bits + [1]:
                if bit < mask & -mask:
                    hand(c, mask, bit).start()
            return 0

        lax.fori_loop(0, parts, pass_on, 0)

    def finish(c, _):
        own(c).wait()
        exchange(c).wait_send()
        for mask in masks:
            hand(c, mask, 1).wait_recv()
            for bit in bits + [1]:
                if mask == 0 or bit < mask & -mask:
                    hand(c, mask, bit).wait_send()
        return 0

    lax.fori_loop(0, parts, finish, 0)
    for k in range(len(masks)):
        cot_copy(k).wait()
        cot_hand(k).wait()


def enter_mlp(ndp, mixed, all_out, tokens, gain, cots):
    rows, features = tokens.shape
    parts, count = rows // PART, len(cots)
    vmem, anywhere = pl.BlockSpec(memory_space=pltpu.VMEM), pl.BlockSpec(memory_space=pl.ANY)
    dma = pltpu.SemaphoreType.DMA
    everyone = jax.ShapeDtypeStruct((ndp, rows, features), bf16)
    low = pltpu.VMEM((rows, features), bf16)
    return pl.pallas_call(
        functools.partial(enter_kernel, ndp),
        out_shape=(jax.ShapeDtypeStruct((rows, features), f32), everyone, everyone),
        in_specs=[vmem] * (4 + count),
        out_specs=(vmem, anywhere, anywhere),
        scratch_shapes=[
            low, low, low, dma((parts,)), dma((parts,)), dma((parts,)), dma((ndp, parts)), dma((ndp, parts)),
            dma((count,)), dma((count,)), dma((count,)),
        ],
        compiler_params=pltpu.CompilerParams(
            collective_id=6, has_side_effects=True, vmem_limit_bytes=VMEM_LIMIT
        ),
        cost_estimate=cost(3),
        name="enter_mlp",
    )(mixed, all_out, tokens, gain, *cots)


def leave_kernel(
    ndp, cots_ref, to_gate_ref, to_up_ref, mixed_ref, gate_up_ref, down_ref, middle_ref, gain_ref,
    grad_gate_ref, grad_up_ref, *refs,
):
    out_refs, refs = refs[: ndp // 2], refs[ndp // 2 :]
    (
        grad_ref, low_ref, gain_out_ref,
    cot_s, to_gate_s, to_up_s, mixed_s, grads_s, out_s, grad_s, load_sem, grads_sem, out_sem, grad_sem,
    keep, core_out, core_in, side_out, side_in, mine, theirs, out_keep, out_core, out_core_in,
    core_sems, side_sems, mp_sems, out_sems,
    ) = refs
    rows, features = middle_ref.shape
    piece = down_ref.shape[1]
    parts = rows // PART
    bits, masks = doubling(ndp)
    dp, z, mp = (lax.axis_index(a) for a in ("dp", "seq", "mp"))
    peers_barrier(ndp)

    def at(c):
        return pl.ds(pl.multiple_of(c * PART, PART), PART)

    def loads(c):
        slot = lax.rem(c, 2)
        pairs = ((cots_ref, cot_s), (to_gate_ref, to_gate_s), (to_up_ref, to_up_s), (mixed_ref, mixed_s))
        return [
            pltpu.make_async_copy(ref.at[:, at(c)], buffer.at[slot], load_sem.at[k, slot])
            for k, (ref, buffer) in enumerate(pairs)
        ]

    def store_grads(c):
        slot = lax.rem(c, 2)
        return [
            pltpu.make_async_copy(
                grads_s.at[slot, :, :, pl.ds(k * piece, piece)], ref.at[:, at(c)], grads_sem.at[slot, k]
            )
            for k, ref in enumerate((grad_gate_ref, grad_up_ref))
        ]

    def store_out(c, k):
        slot = lax.rem(c, 2)
        return pltpu.make_async_copy(out_s.at[slot, k], out_refs[k].at[at(c)], out_sem.at[slot, k])

    def store_grad(c):
        slot = lax.rem(c, 2)
        return pltpu.make_async_copy(grad_s.at[slot], grad_ref.at[at(c)], grad_sem.at[slot])

    def remote(src, dst, sems, index, target):
        return pltpu.make_async_remote_copy(
            src_ref=src, dst_ref=dst, send_sem=sems.at[(0, *index)], recv_sem=sems.at[(1, *index)],
            device_id=target, device_id_type=MESH,
        )

    def to_core(c):
        return remote(core_out.at[lax.rem(c, 2)], core_in.at[c], core_sems, (c,), (flip(dp, 1), z, mp))

    def out_to_core(c):
        return remote(out_core.at[lax.rem(c, 2)], out_core_in.at[c], out_sems, (c,), (flip(dp, 1), z, mp))

    def to_side(c, mask):
        bit = 1 << (mask.bit_length() - 1)
        k = mask // 2 - 1
        return remote(side_out.at[c, k], side_in.at[c, k], side_sems, (c, k), (flip(dp, bit), z, mp))

    def to_mp(c):
        return remote(mine.at[c], theirs.at[c], mp_sems, (c,), (dp, z, 1 - mp))

    for copy in loads(0):
        copy.start()
    gain_out_ref[...] = jnp.zeros_like(gain_out_ref)

    def compute(c):
        slot = lax.rem(c, 2)
        for copy in loads(c):
            copy.wait()

        @pl.when(c + 1 < parts)
        def _():
            for copy in loads(c + 1):
                copy.start()

        @pl.when(c >= 2)
        def _():
            for copy in store_grads(c - 2):
                copy.wait()
            to_core(c - 2).wait_send()
            out_to_core(c - 2).wait_send()

        low_ref[at(c), :] = cot_s[slot, 0]
        grad_mixed = matmul(cot_s[slot].reshape(ndp * PART, features), down_ref[...]).reshape(ndp, PART, piece)
        grads_s[slot, :, :, :piece] = (grad_mixed * to_gate_s[slot].astype(f32)).astype(bf16)
        grads_s[slot, :, :, piece:] = (grad_mixed * to_up_s[slot].astype(f32)).astype(bf16)
        for copy in store_grads(c):
            copy.start()
        total = contract(grads_s[slot].reshape(ndp * PART, 2 * piece), gate_up_ref[...])
        total = total.reshape(ndp, PART, features)
        for mask in range(0, ndp, 2):
            keep[lax.rem(c, 4), mask // 2] = total[mask]
            core_out[slot, mask // 2] = total[mask | 1].astype(bf16)
        to_core(c).start()
        total = contract(mixed_s[slot].reshape(ndp * PART, piece), down_ref[...])
        total = total.reshape(ndp, PART, features)
        for mask in range(0, ndp, 2):
            out_keep[slot, mask // 2] = total[mask]
            out_core[slot, mask // 2] = total[mask | 1].astype(bf16)
        out_to_core(c).start()

    def after_core(c):
        to_core(c).wait_recv()
        slot = lax.rem(c, 4)
        keep[slot, 0] += core_in[c, 0].astype(f32)
        for mask in range(ndp - 2, 0, -2):
            total = keep[slot, mask // 2] + core_in[c, mask // 2].astype(f32)
            bit = 1 << (mask.bit_length() - 1)
            for more in bits:
                if more > bit:
                    to_side(c, mask | more).wait_recv()
                    total = total + side_in[c, (mask | more) // 2 - 1].astype(f32)
            side_out[c, mask // 2 - 1] = total.astype(bf16)
            to_side(c, mask).start()

        @pl.when(c >= 2)
        def _():
            for k in range(ndp // 2):
                store_out(c - 2, k).wait()

        slot = lax.rem(c, 2)
        out_to_core(c).wait_recv()
        for k in range(ndp // 2):
            out_s[slot, k] = (out_keep[slot, k] + out_core_in[c, k].astype(f32)).astype(bf16)
            store_out(c, k).start()

    def after_side(c):
        total = keep[lax.rem(c, 4), 0]
        for bit in bits:
            to_side(c, bit).wait_recv()
            total = total + side_in[c, bit // 2 - 1].astype(f32)
        mine[c] = total.astype(bf16)
        to_mp(c).start()

    def after_mp(c):
        to_mp(c).wait_recv()

        @pl.when(c >= 2)
        def _():
            store_grad(c - 2).wait()

        grad = mine[c].astype(f32) + theirs[c].astype(f32)
        middle = middle_ref[at(c), :]
        scale = lax.rsqrt(jnp.mean(middle * middle, axis=-1, keepdims=True) + epsilon)
        normed = middle * scale
        grad_normed = grad * gain_ref[...]
        grad_middle = low_ref[at(c), :].astype(f32) + scale * (
            grad_normed - normed * jnp.mean(grad_normed * normed, axis=-1, keepdims=True)
        )
        grad_s[lax.rem(c, 2)] = grad_middle
        store_grad(c).start()
        low_ref[at(c), :] = grad_middle.astype(bf16)
        gain_out_ref[...] += jnp.sum((grad * normed).reshape(PART // 8, 8, features), axis=0)

    def turn(t, _):
        for lag, stage in ((0, compute), (1, after_core), (2, after_side), (4, after_mp)):
            pl.when((t >= lag) & (t < parts + lag))(functools.partial(stage, t - lag))
        return 0

    lax.fori_loop(0, parts + 4, turn, 0)
    for c in (parts - 2, parts - 1):
        for copy in store_grads(c):
            copy.wait()
        for k in range(ndp // 2):
            store_out(c, k).wait()
        store_grad(c).wait()
        to_core(c).wait_send()
        out_to_core(c).wait_send()

    def finish(c, _):
        to_mp(c).wait_send()
        for mask in range(2, ndp, 2):
            to_side(c, mask).wait_send()
        return 0

    lax.fori_loop(0, parts, finish, 0)


def leave_mlp(ndp, cots, to_gate, to_up, mixed, gate_up, down, middle, gain):
    rows, features = middle.shape
    piece = down.shape[1]
    parts, evens = rows // PART, ndp // 2
    vmem, anywhere = pl.BlockSpec(memory_space=pltpu.VMEM), pl.BlockSpec(memory_space=pl.ANY)
    dma = pltpu.SemaphoreType.DMA
    low = functools.partial(pltpu.VMEM, dtype=bf16)
    thin = (parts, PART, features)
    return pl.pallas_call(
        functools.partial(leave_kernel, ndp),
        out_shape=(
            *[jax.ShapeDtypeStruct((ndp, rows, piece), bf16)] * 2,
            *[jax.ShapeDtypeStruct((rows, features), bf16)] * evens,
            jax.ShapeDtypeStruct((rows, features), f32),
            jax.ShapeDtypeStruct((rows, features), bf16),
            jax.ShapeDtypeStruct((8, features), f32),
        ),
        in_specs=[anywhere] * 4 + [vmem] * 4,
        out_specs=(*[anywhere] * (3 + evens), vmem, vmem),
        scratch_shapes=[
            low((2, ndp, PART, features)),
            pltpu.VMEM((2, ndp, PART, piece), to_gate.dtype),
            pltpu.VMEM((2, ndp, PART, piece), to_up.dtype),
            low((2, ndp, PART, piece)),
            low((2, ndp, PART, 2 * piece)),
            low((2, evens, PART, features)),
            pltpu.VMEM((2, PART, features), f32),
            dma((4, 2)), dma((2, 2)), dma((2, evens)), dma((2,)),
            pltpu.VMEM((4, evens, PART, features), f32),
            low((2, evens, PART, features)), low((parts, evens, PART, features)),
            low((parts, evens - 1, PART, features)), low((parts, evens - 1, PART, features)),
            low(thin), low(thin),
            pltpu.VMEM((2, evens, PART, features), f32),
            low((2, evens, PART, features)), low((parts, evens, PART, features)),
            dma((2, parts)), dma((2, parts, evens - 1)), dma((2, parts)), dma((2, parts)),
        ],
        compiler_params=pltpu.CompilerParams(
            collective_id=7, has_side_effects=True, vmem_limit_bytes=VMEM_LIMIT
        ),
        cost_estimate=cost(3),
        name="leave_mlp",
    )(cots, to_gate, to_up, mixed, gate_up, down, middle, gain)


def everyone(ndp, values):
    masks = doubling(ndp)[1]
    by_mask = {}
    for mask, value in zip(masks, values):
        by_mask[mask], by_mask[mask | 1] = value, xor_permute(value, "dp", 1)
    return jnp.stack([by_mask[mask] for mask in range(ndp)])


def side_sum(ndp, value):
    return list((value[0::2].astype(f32) + xor_permute(value[1::2], "dp", 1).astype(f32)).astype(bf16))


def halving(ndp, values, after=None):
    for bit in doubling(ndp)[0]:
        half = len(values) // 2
        others = [xor_permute(value, "dp", bit) for value in values[half:]]
        if after is not None:
            others, _ = lax.optimization_barrier((others, after))
        values = [
            (value.astype(f32) + other.astype(f32)).astype(bf16) for value, other in zip(values[:half], others)
        ]
    return values[0]


def enter_mlp_plain(ndp, mixed, all_out, tokens, gain, cots):
    part = contract(mixed, all_out).astype(bf16)
    middle = tokens.astype(f32) + (part.astype(f32) + xor_permute(part, "mp", 1).astype(f32))
    normed = [(middle * norm_scale(middle) * gain).astype(bf16)]
    for bit in doubling(ndp)[0]:
        normed += [xor_permute(value, "dp", bit) for value in normed]
    return middle, everyone(ndp, normed), everyone(ndp, cots)


def leave_mlp_plain(ndp, cots, to_gate, to_up, mixed, gate_up, down, middle, gain):
    rows, features = middle.shape
    piece = down.shape[1]
    grad_mixed = matmul(cots.reshape(-1, features), down).reshape(ndp, rows, piece)
    grads = jnp.concatenate([grad_mixed * to_gate, grad_mixed * to_up], axis=-1).astype(bf16)
    total = contract(grads.reshape(-1, 2 * piece), gate_up).astype(bf16).reshape(ndp, rows, features)
    total = halving(ndp, side_sum(ndp, total))
    grad = total.astype(f32) + xor_permute(total, "mp", 1).astype(f32)
    scale = norm_scale(middle)
    normed, grad_normed = middle * scale, grad * gain
    grad_middle = cots[0].astype(f32) + scale * (
        grad_normed - normed * jnp.mean(grad_normed * normed, axis=-1, keepdims=True)
    )
    out = contract(mixed.reshape(-1, piece), down).astype(bf16).reshape(ndp, rows, features)
    gain_out = jnp.sum((grad * normed).reshape(rows // 8, 8, features), axis=0)
    return grads[..., :piece], grads[..., piece:], *side_sum(ndp, out), grad_middle, grad_middle.astype(bf16), gain_out


def on_device(
    ndp, nseq,
    tokens, doc_lengths, norm_gain, w_y, w_x, gate_a, gate_i, bias_a, bias_i, conv_w, conv_b,
    decay_param, w_out, mlp_gain, w_gate, w_up, w_down, cotangent,
):
    local_len, features = tokens.shape
    rows_here = w_y.shape[0]
    hidden_here = w_gate.shape[1]
    block = gate_a.shape[1]
    piece = hidden_here // ndp
    bits = [1 << k for k in range(ndp.bit_length() - 1)]

    def spread(value):
        values = [value]
        for bit in doubling(ndp)[0]:
            values += [xor_permute(v, "dp", bit) for v in values]
        return values

    def flat(value):
        return value.reshape(-1, value.shape[-1])

    (all_y, all_x, all_out), gate_up_rows, all_down, acts_one, acts_one_t = gather_weights(
        ndp, nseq, tokens, norm_gain[None], [w_y, w_x, w_out], [w_gate, w_up, w_down]
    )
    gate_up = lax.all_gather(gate_up_rows.reshape(ndp, rows_here, -1), "seq", axis=1, tiled=True)
    gate_up = gate_up.reshape(features, -1)

    position = lax.axis_index("seq") * local_len + jnp.arange(local_len + PAD, dtype=jnp.int32)
    lengths_row = doc_lengths[0]
    starts = jnp.cumsum(lengths_row) - lengths_row
    resets = jnp.any(position[:, None] == starts[None, :], axis=1)
    doc_start = jnp.max(jnp.where(starts[None, :] <= position[:, None], starts[None, :], 0), axis=1)
    marks = jnp.stack(
        [1.0 - resets.astype(f32)] + [(position - lag >= doc_start).astype(f32) for lag in (1, 2, 3)]
    )
    marks = jnp.broadcast_to(marks[:, :, None], (4, local_len + PAD, LANES))
    vectors = jnp.concatenate(
        [conv_w, conv_b[None], bias_a[None], bias_i[None], jax.nn.softplus(-decay_param)[None]], axis=0
    )

    cots_ready, _ = lax.optimization_barrier((cotangent, all_y))
    mixed_rec, states, pxe, pre_y, rate, ig, conv_out = rec_forward(
        nseq, acts_one, all_x, all_y, marks, gate_a, gate_i, vectors
    )
    all_cots = spread(cots_ready)

    small_group = ndp <= 4
    middle, acts, cots = (enter_mlp if small_group else enter_mlp_plain)(
        ndp, mixed_rec, all_out, tokens, mlp_gain[None], all_cots
    )
    acts_flat, cots_flat = flat(acts), flat(cots)
    pre = matmul(acts_flat, gate_up)
    pre_gate, pre_up = pre[:, :piece], pre[:, piece:]
    gelu, slope = gelu_parts(pre_gate)
    mixed = (gelu * pre_up).astype(bf16)
    to_gate, to_up = (pre_up * slope).reshape(ndp, local_len, piece), gelu.reshape(ndp, local_len, piece)

    def rows_total(left, right):
        return contract_rows(left, right).astype(bf16).reshape(ndp, nseq * rows_here, -1)

    def reduce_mlp(total):
        return lax.psum_scatter(total, "seq", scatter_dimension=1, tiled=True)

    total_down, mixed = lax.optimization_barrier((rows_total(cots_flat, mixed), mixed))
    sum_down = reduce_mlp(total_down)
    grad_gate, grad_up, *out_sides, grad_middle, grad_middle_low, gain_two = (leave_mlp if small_group else leave_mlp_plain)(
        ndp, cots, to_gate, to_up, mixed.reshape(ndp, local_len, piece), gate_up, all_down, middle, mlp_gain[None]
    )
    total_gate = rows_total(acts_flat, flat(grad_gate))
    total_up = rows_total(acts_flat, flat(grad_up))
    total_gate, total_up, grad_middle_low, sum_down = lax.optimization_barrier(
        (total_gate, total_up, grad_middle_low, sum_down)
    )
    sum_gate, sum_up = reduce_mlp(total_gate), reduce_mlp(total_up)

    grad_pre_y, grad_pre_x, grad_gate_a, grad_gate_i, sums, grad_w_out = rec_backward(
        ndp, nseq, grad_middle_low, mixed_rec, all_out, marks, gate_a, gate_i, vectors,
        (pre_y, states, rate, pxe, ig, conv_out),
    )
    part = (contract(grad_pre_y, all_y) + contract(grad_pre_x, all_x)).astype(bf16)
    other = xor_permute(part, "mp", 1)
    out_part = halving(ndp, out_sides, grad_pre_y)
    other_out = xor_permute(out_part, "mp", 1)
    resid = tokens.astype(f32)
    scale_one = norm_scale(resid)
    normed = resid * scale_one
    small = [
        grad_gate_a, grad_gate_i, sums, jnp.sum(part.astype(f32) * normed, axis=0), jnp.sum(gain_two, axis=0),
    ]
    sizes = [value.size // block for value in small]
    total_rows = -(-sum(sizes) // (16 * ndp * nseq)) * 16 * ndp * nseq
    small_rows = jnp.concatenate(
        [value.reshape(-1, block) for value in small] + [jnp.zeros((total_rows - sum(sizes), block), f32)], axis=0
    )
    moved = [] if piece % LANES else [sum_gate, sum_down]
    small_all, grad_w_y, grad_w_x, grad_w_out, *moved = reduce_weights(
        ndp, nseq, [acts_one_t], [(None, small_rows), (0, grad_pre_y), (0, grad_pre_x), (-1, grad_w_out)], moved
    )
    small_all, sum_up, other, other_out = lax.optimization_barrier((small_all, sum_up, other, other_out))
    totals, begin = [], 0
    for value, size in zip(small, sizes):
        totals.append(small_all[begin : begin + size].astype(f32).reshape(value.shape))
        begin += size
    grad_gate_a, grad_gate_i, sums, gain_one, gain_two = totals
    gain_one = gain_one + xor_permute(gain_one, "mp", 1)

    grad_acts = part.astype(f32) + other.astype(f32)
    grad_normed = grad_acts * norm_gain
    input_grad = grad_middle + scale_one * (
        grad_normed - normed * jnp.mean(grad_normed * normed, axis=-1, keepdims=True)
    )

    output = (middle + (out_part.astype(f32) + other_out.astype(f32))).astype(bf16)

    grad_w_gate, grad_w_down = moved or [regroup_plain(sum_gate), regroup_plain(sum_down)]
    (grad_w_up,) = regroup(ndp, [sum_up])
    return (
        output,
        input_grad,
        gain_one,
        grad_w_y,
        grad_w_x,
        grad_gate_a,
        grad_gate_i,
        sums[0],
        sums[1],
        sums[4:8],
        sums[3],
        sums[2] * jax.nn.sigmoid(-decay_param),
        grad_w_out,
        gain_two,
        grad_w_gate,
        grad_w_up,
        grad_w_down,
    )


def solution(mesh):
    rows, cols = P(("dp", "seq"), None), P(("dp", "seq"), "mp")
    return jax.shard_map(
        functools.partial(on_device, mesh.shape["dp"], mesh.shape["seq"]),
        mesh=mesh,
        in_specs=(
            rows, P("dp", None), P(), cols, cols, P("mp", None, None), P("mp", None, None), P("mp"), P("mp"),
            P(None, "mp"), P("mp"), P("mp"), cols, P(), cols, cols, cols, rows,
        ),
        out_specs=(
            rows, rows, P(), cols, cols, P("mp", None, None), P("mp", None, None), P("mp"), P("mp"),
            P(None, "mp"), P("mp"), P("mp"), cols, P(), cols, cols, cols,
        ),
        check_vma=False,
    )
```
